32 devices in a mesh: ctx: 8 (over z, x), tp: 4 (over y, core).
Axes of the slice: x: 2, y: 2, z: 4, core: 2. Of those that a mesh axis runs over, the one named last changes fastest.
Arguments:
- queries: bfloat16 [1024, 1024], P('ctx', 'tp'), may hold values from -5 to 5
- key_states: bfloat16 [1024, 1024], P('ctx', 'tp'), may hold values from -5 to 5
- value_states: bfloat16 [1024, 1024], P('ctx', 'tp'), may hold values from -6 to 6
- attn_output: bfloat16 [1024, 1024], P('ctx', 'tp'), may hold values from -6 to 6
- output_grad: bfloat16 [1024, 1024], P('ctx', 'tp'), may hold values from -6 to 6
- block_map: int32 [8, 8], replicated, may hold values from 0 to 1, as said below
- w_query: bfloat16 [8192, 1024], P('ctx', 'tp'), may hold values from -0.1875 to 0.1875
- w_key: bfloat16 [8192, 1024], P('ctx', 'tp'), may hold values from -0.1875 to 0.1875
- w_value: bfloat16 [8192, 1024], P('ctx', 'tp'), may hold values from -0.1875 to 0.1875
Outputs:
- grad_input: bfloat16 [1024, 8192], P('tp', 'ctx')
The draws below stay inside these ranges and needn't reach their ends.
Inputs may be any that keep to these rules, and one draw needn't show every extreme that they name: block_map[i, j] is 1 wherever |i - j| <= 1; elsewhere each row is 1 on a share of its entries that differs from row to row.
All inputs are finite; a program needn't handle non-finite values.
Results may differ from the reference program's by a relative error of at most 0.014.
Values may be sent and summed in bfloat16 or wider, within the bound.
A program may use at most 64 MiB of HBM per device.

```python
import math
import jax
import jax.numpy as jnp
from jax import lax

D = 8192
HD = 128
HEADS_DEV = 2
BLK = 128
SLAB = 128
TOKENS = 1024
HEADS = 8
HC = 1024
N_CTX = 8
N_TP = 4


def draw_queries(key, part):
    base = jnp.clip(jax.random.normal(jax.random.fold_in(key, 1), (TOKENS, HC), jnp.float32), -5.0, 5.0)
    return base.astype(jnp.bfloat16)


def draw_key_states(key, part):
    base = jnp.clip(jax.random.normal(jax.random.fold_in(key, 2), (TOKENS, HC), jnp.float32), -5.0, 5.0)
    return base.astype(jnp.bfloat16)


def draw_block_map(key, part):
    count = TOKENS // BLK
    density = jax.random.randint(jax.random.fold_in(key, 5), (count, 1), 1, 16)
    coins = jax.random.randint(jax.random.fold_in(key, 6), (count, count), 0, 16)
    rows = jnp.arange(count)
    near = jnp.abs(rows[:, None] - rows[None, :]) <= 1
    return jnp.where(near | (coins < density), 1, 0).astype(jnp.int32)


def levels(key, shape, split, smallest, largest):
    def one(axis_at, blocks):
        heights = jax.random.uniform(jax.random.fold_in(jax.random.fold_in(key, 6), axis_at), (blocks,), jnp.float32, smallest / len(split), largest / len(split))
        return jnp.repeat(jnp.exp(heights), shape[axis_at] // blocks).reshape((-1,) + (1,) * (len(shape) - axis_at - 1))

    level = one(*split[0])
    for cut in split[1:]:
        level = level * one(*cut)
    return level


def normal_values(own_key, shape, scale, most, shards=(), held_as=jnp.bfloat16):
    entries = jax.random.normal(own_key, shape, jnp.float32) * scale
    if len(shards) > 0:
        entries = levels(own_key, shape, shards, -0.22, 0.18) * entries
    return jnp.clip(entries, min=-most, max=most).astype(held_as)


def setup_inputs(seed: int = 0) -> dict:
    seeds = jax.random.split(jax.random.key(seed), 10)
    return {
        "queries": draw_queries(jax.random.fold_in(seeds[9], 71), 0),
        "key_states": draw_key_states(jax.random.fold_in(seeds[9], 71), 0),
        "value_states": normal_values(seeds[2], (TOKENS, HC), 1.0, 6.0, ((0, 8), (1, 4))),
        "attn_output": normal_values(seeds[3], (TOKENS, HC), 1.0, 6.0, ((0, 8), (1, 4))),
        "output_grad": normal_values(seeds[4], (TOKENS, HC), 1.0, 6.0, ((0, 8), (1, 4))),
        "block_map": draw_block_map(jax.random.fold_in(seeds[9], 71), 0),
        "w_query": normal_values(seeds[6], (D, HC), HC ** -0.5, 0.1875, ((0, 8), (1, 4))),
        "w_key": normal_values(seeds[7], (D, HC), HC ** -0.5, 0.1875, ((0, 8), (1, 4))),
        "w_value": normal_values(seeds[8], (D, HC), HC ** -0.5, 0.1875, ((0, 8), (1, 4))),
    }


NEG_FILL = -1e+30

def expand_map(block_map):
    count = block_map.shape[0]
    spread = jnp.broadcast_to(block_map[:, None, :, None], (count, BLK, count, BLK))
    return spread.reshape(count * BLK, count * BLK) > 0

def resolved_rows(values):
    return lax.optimization_barrier(values.astype(jnp.bfloat16)).astype(jnp.float32)

def head_grads(head_index, queries, key_states, value_states, attn_output, output_grad, allowed):

    def columns(array):
        return lax.dynamic_slice_in_dim(array, head_index * HD, HD, 1)
    query_head = columns(queries)
    key_head_index = columns(key_states)
    value_head = columns(value_states)
    output_head = columns(attn_output)
    grad_head = columns(output_grad)
    score_scale = 1.0 / math.sqrt(HD)
    scores = jnp.dot(query_head, key_head_index.T, preferred_element_type=jnp.float32) * score_scale
    masked = jnp.where(allowed, scores, NEG_FILL)
    row_max = lax.optimization_barrier(jnp.max(masked, axis=1, keepdims=True))
    row_sum = lax.optimization_barrier(jnp.sum(jnp.where(allowed, jnp.exp(masked - row_max), 0.0), axis=1, keepdims=True))
    log_total = row_max + jnp.log(row_sum)
    probs = jnp.where(allowed, jnp.exp(masked - log_total), 0.0)
    probs_low = probs.astype(jnp.bfloat16)
    dprobs = jnp.dot(grad_head, value_head.T, preferred_element_type=jnp.float32)
    row_delta = lax.optimization_barrier(jnp.sum(grad_head.astype(jnp.float32) * output_head.astype(jnp.float32), axis=1, keepdims=True))
    score_gradient = (probs * (dprobs - row_delta) * score_scale).astype(jnp.bfloat16)

    def split_rows(matrix):
        return matrix.astype(jnp.float32).reshape(N_CTX, SLAB, N_CTX, SLAB)

    def rows_for_part(array):
        return array.astype(jnp.float32).reshape(N_CTX, SLAB, HD)
    grad_v = lax.optimization_barrier(jnp.sum(resolved_rows(jnp.einsum('aqbk,aqd->abkd', split_rows(probs_low), rows_for_part(grad_head))), axis=0))
    grad_k = lax.optimization_barrier(jnp.sum(resolved_rows(jnp.einsum('aqbk,aqd->abkd', split_rows(score_gradient), rows_for_part(query_head))), axis=0))
    query_gradient = lax.optimization_barrier(jnp.sum(resolved_rows(jnp.einsum('hpru,rug->hrpg', split_rows(score_gradient), rows_for_part(key_head_index))), axis=1))
    return (query_gradient.reshape(TOKENS, HD).astype(jnp.bfloat16), grad_k.reshape(TOKENS, HD).astype(jnp.bfloat16), grad_v.reshape(TOKENS, HD).astype(jnp.bfloat16))

def reference(queries, key_states, value_states, attn_output, output_grad, block_map, w_query, w_key, w_value):
    allowed = expand_map(block_map)

    def one_head(head_index):
        return head_grads(head_index, queries, key_states, value_states, attn_output, output_grad, allowed)
    query_gradient, grad_k, grad_v = lax.map(one_head, jnp.arange(HEADS, dtype=jnp.int32))

    def joined(stack):
        return jnp.transpose(stack, (1, 0, 2)).reshape(TOKENS, HEADS * HD)
    query_gradient, grad_k, grad_v = (joined(query_gradient), joined(grad_k), joined(grad_v))
    group_width = HEADS_DEV * HD

    def group_step(summed, group_index):

        def columns(array):
            return lax.dynamic_slice_in_dim(array, group_index * group_width, group_width, 1)
        term = jnp.dot(columns(query_gradient), columns(w_query).T, preferred_element_type=jnp.float32)
        term = term + jnp.dot(columns(grad_k), columns(w_key).T, preferred_element_type=jnp.float32)
        term = term + jnp.dot(columns(grad_v), columns(w_value).T, preferred_element_type=jnp.float32)
        return (summed + resolved_rows(term), None)
    summed, _ = lax.scan(group_step, jnp.zeros((TOKENS, D), jnp.float32), jnp.arange(N_TP, dtype=jnp.int32))
    return summed.astype(jnp.bfloat16)
```

```python
import functools
import math

import jax
import jax.numpy as jnp
from jax import lax
from jax.experimental import pallas as pl
from jax.experimental.pallas import tpu as pltpu
from jax.sharding import PartitionSpec as P

HD = 128
BLK = 128


NEG_FILL = -1e30


def block_mask(block_map, row_offset, row_count, col_offset, col_count):
    tiles = lax.dynamic_slice(
        block_map, (row_offset // BLK, col_offset // BLK), (row_count // BLK, col_count // BLK)
    )
    spread = jnp.broadcast_to(
        tiles[:, None, :, None], (row_count // BLK, BLK, col_count // BLK, BLK)
    )
    return spread.reshape(row_count, col_count) > 0


def resolved_rows(values):
    return lax.optimization_barrier(values.astype(jnp.bfloat16)).astype(jnp.float32)


def stat_update(state, query_heads, key_block, allowed, score_scale):
    row_max, row_sum = state
    scores = (
        jnp.einsum("qhd,khd->hqk", query_heads, key_block, preferred_element_type=jnp.float32)
        * score_scale
    )
    masked = jnp.where(allowed[None], scores, NEG_FILL)
    new_max = jnp.maximum(row_max, jnp.max(masked, axis=2))
    kept = jnp.where(allowed[None], jnp.exp(masked - new_max[:, :, None]), 0.0)
    return (new_max, row_sum * jnp.exp(row_max - new_max) + jnp.sum(kept, axis=2))


def gradient_block(
    query_heads, grad_heads, key_block, value_block, log_total, row_delta, allowed, score_scale
):
    scores = (
        jnp.einsum("qhd,khd->hqk", query_heads, key_block, preferred_element_type=jnp.float32)
        * score_scale
    )
    masked = jnp.where(allowed[None], scores, NEG_FILL)
    probs = jnp.where(allowed[None], jnp.exp(masked - log_total[:, :, None]), 0.0)
    probs_low = probs.astype(jnp.bfloat16)
    dprobs = jnp.einsum("qhd,khd->hqk", grad_heads, value_block, preferred_element_type=jnp.float32)
    score_gradient = (probs * (dprobs - row_delta[:, :, None]) * score_scale).astype(jnp.bfloat16)
    return (probs_low, score_gradient)


def per_device(
    queries, key_states, value_states, attn_output, output_grad, block_map, w_query, w_key, w_value
):
    slab_rows, width = queries.shape
    head_count = width // HD
    context_count = lax.axis_size("ctx")
    score_scale = 1.0 / math.sqrt(HD)
    row_offset = lax.axis_index("ctx") * slab_rows
    query_heads = queries.reshape(slab_rows, head_count, HD)
    grad_heads = output_grad.reshape(slab_rows, head_count, HD)
    output_heads = attn_output.reshape(slab_rows, head_count, HD)
    row_delta = jnp.sum(grad_heads.astype(jnp.float32) * output_heads.astype(jnp.float32), axis=2).T
    start_state = (
        jnp.full((head_count, slab_rows), NEG_FILL, jnp.float32),
        jnp.zeros((head_count, slab_rows), jnp.float32),
    )
    full_keys, full_values = (
        lax.all_gather(key_states, "ctx", axis=0, tiled=True),
        lax.all_gather(value_states, "ctx", axis=0, tiled=True),
    )
    group_size = min(context_count, max(1, 512 // slab_rows))
    key_span = slab_rows * group_size
    total_block_count = context_count // group_size
    key_blocks = full_keys.reshape(total_block_count, key_span, head_count, HD)
    value_blocks = full_values.reshape(total_block_count, key_span, head_count, HD)
    block_ids = jnp.arange(total_block_count, dtype=jnp.int32)

    def stat_step(state, inputs):
        key_block, block_index = inputs
        allowed = block_mask(block_map, row_offset, slab_rows, block_index * key_span, key_span)

        def stat_active_step(previous):
            return stat_update(previous, query_heads, key_block, allowed, score_scale)

        return (
            lax.cond(jnp.any(allowed), stat_active_step, lambda previous: previous, state),
            None,
        )

    (row_max, row_sum), _ = lax.scan(stat_step, start_state, (key_blocks, block_ids))
    log_total = row_max + jnp.log(row_sum)

    def back_step(dq_total, inputs):
        key_block, value_block, block_index = inputs
        allowed = block_mask(block_map, row_offset, slab_rows, block_index * key_span, key_span)

        def back_active_step(previous):
            probs_low, score_gradient = gradient_block(
                query_heads,
                grad_heads,
                key_block,
                value_block,
                log_total,
                row_delta,
                allowed,
                score_scale,
            )
            dv_part = jnp.einsum(
                "hqk,qhd->khd", probs_low, grad_heads, preferred_element_type=jnp.float32
            ).astype(jnp.bfloat16)
            dk_part = jnp.einsum(
                "hqk,qhd->khd", score_gradient, query_heads, preferred_element_type=jnp.float32
            ).astype(jnp.bfloat16)
            per_slab = jnp.einsum(
                "hqgk,gkhd->gqhd",
                score_gradient.reshape(head_count, slab_rows, group_size, slab_rows),
                key_block.reshape(group_size, slab_rows, head_count, HD),
                preferred_element_type=jnp.float32,
            )
            joined = jnp.concatenate(
                [dk_part.reshape(key_span, width), dv_part.reshape(key_span, width)], axis=1
            )
            return (previous + jnp.sum(resolved_rows(per_slab), axis=0), joined)

        def empty_step(previous):
            return (previous, jnp.zeros((key_span, 2 * width), jnp.bfloat16))

        return lax.cond(jnp.any(allowed), back_active_step, empty_step, dq_total)

    dq_total, joined_blocks = lax.scan(
        back_step,
        jnp.zeros((slab_rows, head_count, HD), jnp.float32),
        (key_blocks, value_blocks, block_ids),
    )
    local_grads = dq_total.astype(jnp.bfloat16).reshape(slab_rows, width)
    part_grads = joined_blocks.reshape(context_count * slab_rows, 2 * width)
    part_width = part_grads.shape[1]
    arrived = lax.all_to_all(
        part_grads.reshape(context_count, slab_rows, part_width),
        "ctx",
        split_axis=0,
        concat_axis=0,
        tiled=True,
    )
    finished = jnp.sum(arrived.astype(jnp.float32), axis=0).astype(jnp.bfloat16)
    own_grads = jnp.concatenate([local_grads, finished], axis=1)
    gradients = lax.all_gather(own_grads, "ctx", axis=0, tiled=True)
    projections = jnp.concatenate([w_query, w_key, w_value], axis=1)
    return lax.psum_scatter(
        lax.dot_general(
            gradients, projections, (((1,), (1,)), ((), ())), preferred_element_type=jnp.float32
        ).astype(jnp.bfloat16),
        "tp",
        scatter_dimension=0,
        tiled=True,
    )


MESH = pl.DeviceIdType.MESH
LOG2E = 1.4426950408889634
PAIR = 2 * BLK
CHUNK = 4 * BLK + 16
PIECE = 256


def contract(a, b, da, db):
    return lax.dot_general(a, b, (((da,), (db,)), ((), ())), preferred_element_type=jnp.float32)


def fused_kernel(
    n,
    q_ref,
    k_ref,
    v_ref,
    o_ref,
    g_ref,
    map_ref,
    wq_hbm,
    wk_hbm,
    wv_hbm,
    out_ref,
    held,
    bias,
    dk_acc,
    dv_acc,
    grads,
    w_ref,
    to_sib,
    from_sib,
    to_far,
    from_far,
    w_sem,
    ctx_send,
    ctx_recv,
    sib_send,
    sib_recv,
    far_send,
    far_recv,
):
    heads = q_ref.shape[1] // HD
    depth = n // 2
    tokens = n * BLK
    pieces = to_far.shape[0]
    block_rows = to_far.shape[1]
    c = lax.axis_index("ctx")
    t = lax.axis_index("tp")
    z = c // 2
    other = c + 1 - 2 * (c % 2)
    sib = t + 1 - 2 * (t % 2)
    far = (t + 2) % 4
    scale = 1.0 / math.sqrt(HD)

    barrier = pltpu.get_barrier_semaphore()
    for peer in ({"ctx": other}, {"tp": sib}, {"tp": far}):
        pl.semaphore_signal(barrier, inc=1, device_id=peer, device_id_type=MESH)

    @pl.when(z > 0)
    def _():
        pl.semaphore_signal(barrier, inc=1, device_id={"ctx": c - 2}, device_id_type=MESH)

    @pl.when(z < depth - 1)
    def _():
        pl.semaphore_signal(barrier, inc=1, device_id={"ctx": c + 2}, device_id_type=MESH)

    w_copies = [
        pltpu.make_async_copy(w, w_ref.at[:, pl.ds(i * heads * HD, heads * HD)], w_sem.at[i])
        for i, w in enumerate((wq_hbm, wk_hbm, wv_hbm))
    ]
    for copy in w_copies:
        copy.start()

    for h in range(heads):
        cols = slice(h * HD, (h + 1) * HD)
        held[h, c, 0:BLK, :] = q_ref[:, cols]
        held[h, c, BLK : 2 * BLK, :] = k_ref[:, cols]
        held[h, c, 2 * BLK : 3 * BLK, :] = v_ref[:, cols]
        held[h, c, 3 * BLK : 4 * BLK, :] = g_ref[:, cols]
        product = g_ref[:, cols].astype(jnp.float32) * o_ref[:, cols].astype(jnp.float32)
        delta = jnp.sum(product.T, axis=0, keepdims=True)
        high = delta.astype(jnp.bfloat16)
        rest = delta - high.astype(jnp.float32)
        middle = rest.astype(jnp.bfloat16)
        low = (rest - middle.astype(jnp.float32)).astype(jnp.bfloat16)
        held[h, c, 4 * BLK : CHUNK, :] = jnp.concatenate(
            [high, middle, low, jnp.zeros((CHUNK - 4 * BLK - 3, BLK), jnp.bfloat16)], axis=0
        )

    def ctx_copy(h, slab, way, target):
        return pltpu.make_async_remote_copy(
            src_ref=held.at[h, slab],
            dst_ref=held.at[h, slab],
            send_sem=ctx_send.at[h, way, slab],
            recv_sem=ctx_recv.at[h, slab],
            device_id={"ctx": target},
            device_id_type=MESH,
        )

    def send_up(h, slab):
        @pl.when(z < depth - 1)
        def _():
            ctx_copy(h, slab, 0, c + 2).start()

    def send_down(h, slab):
        @pl.when(z > 0)
        def _():
            ctx_copy(h, slab, 1, c - 2).start()

    def send_own(h):
        send_up(h, c)
        send_down(h, c)
        ctx_copy(h, c, 2, other).start()

    def pass_on(h, d):
        @pl.when(z - d >= 0)
        def _():
            slab = c - 2 * d
            ctx_copy(h, slab, 0, c).wait_recv()
            send_up(h, slab)
            ctx_copy(h, slab, 2, other).start()

        @pl.when(z + d < depth)
        def _():
            slab = c + 2 * d
            ctx_copy(h, slab, 0, c).wait_recv()
            send_down(h, slab)
            ctx_copy(h, slab, 2, other).start()

    pl.semaphore_wait(
        barrier,
        3 + jnp.where(z > 0, 1, 0) + jnp.where(z < depth - 1, 1, 0),
    )
    send_own(0)
    send_own(1)

    for a in range(n):
        for b in range(n):
            bias[b : b + 1, a * BLK : (a + 1) * BLK] = jnp.full(
                (1, BLK), jnp.where(map_ref[a, b] > 0, 0.0, NEG_FILL), jnp.float32
            )

    def attend(h, i):
        first = 2 * i
        keys = held[h, :, BLK : 2 * BLK, :].reshape(tokens, HD)
        values = held[h, :, 2 * BLK : 3 * BLK, :].reshape(tokens, HD)
        pair_q = held[h, pl.ds(first, 2), 0:BLK, :].reshape(PAIR, HD)
        pair_g = held[h, pl.ds(first, 2), 3 * BLK : 4 * BLK, :].reshape(PAIR, HD)
        tails = held[h, pl.ds(first, 2), 4 * BLK : CHUNK, :].astype(jnp.float32)
        sums = jnp.sum(tails, axis=1)
        delta = jnp.concatenate([sums[0:1], sums[1:2]], axis=1)
        columns = pl.ds(pl.multiple_of(i * PAIR, PAIR), PAIR)
        scores = contract(keys, pair_q, 1, 1) * (scale * LOG2E)
        masked = scores.reshape(n, BLK, PAIR) + bias[:, columns][:, None, :]
        top = jnp.max(masked, axis=(0, 1), keepdims=True)
        raised = jnp.exp2(masked - top)
        total = jnp.sum(raised, axis=(0, 1), keepdims=True)
        probs = (raised * (1.0 / total)).reshape(tokens, PAIR)
        dprobs = contract(values, pair_g, 1, 1)
        dscores = (probs * (dprobs - delta)).astype(jnp.bfloat16)
        probs_low = probs.astype(jnp.bfloat16)
        dv_part = contract(probs_low, pair_g, 1, 0)
        dk_part = contract(dscores, pair_q, 1, 0)
        dv_acc[...] += dv_part
        dk_acc[...] += dk_part
        dq = contract(dscores, keys, 0, 0) * scale
        grads[pl.ds(pl.multiple_of(i * PAIR, PAIR), PAIR), h * HD : (h + 1) * HD] = dq.astype(
            jnp.bfloat16
        )

    def finish_head(h):
        base = heads * HD
        grads[:, base + h * HD : base + (h + 1) * HD] = (dk_acc[...] * scale).astype(jnp.bfloat16)
        grads[:, 2 * base + h * HD : 2 * base + (h + 1) * HD] = dv_acc[...].astype(jnp.bfloat16)

    def clear():
        dk_acc[...] = jnp.zeros_like(dk_acc)
        dv_acc[...] = jnp.zeros_like(dv_acc)

    def passive(h):
        def one(j, carry):
            ctx_copy(h, (1 - c % 2) + 2 * j, 0, c).wait_recv()
            return carry

        lax.fori_loop(0, depth, one, 0)

    for d in range(1, depth):
        pass_on(0, d)
    passive(0)
    clear()

    def first_head(i, carry):
        @pl.when(i >= 1)
        def _():
            pass_on(1, i)

        attend(0, i)
        return carry

    lax.fori_loop(0, n // 2, first_head, 0)
    finish_head(0)
    passive(1)
    clear()

    def second_head(i, carry):
        attend(1, i)
        return carry

    lax.fori_loop(0, n // 2, second_head, 0)
    finish_head(1)
    for copy in w_copies:
        copy.wait()

    def term(block, p):
        rows = grads[pl.ds(pl.multiple_of(block * block_rows, block_rows), block_rows), :]
        return contract(rows, w_ref[pl.ds(pl.multiple_of(p * PIECE, PIECE), PIECE), :], 1, 1)

    def sib_copy(k, p):
        return pltpu.make_async_remote_copy(
            src_ref=to_sib.at[k, p],
            dst_ref=from_sib.at[k, p],
            send_sem=sib_send.at[k, p],
            recv_sem=sib_recv.at[k, p],
            device_id={"tp": sib},
            device_id_type=MESH,
        )

    def far_copy(p):
        return pltpu.make_async_remote_copy(
            src_ref=to_far.at[p],
            dst_ref=from_far.at[p],
            send_sem=far_send.at[p],
            recv_sem=far_recv.at[p],
            device_id={"tp": far},
            device_id_type=MESH,
        )

    def for_sib(k, block):
        def one(p, carry):
            to_sib[k, p] = term(block, p).astype(jnp.bfloat16)
            sib_copy(k, p).start()
            return carry

        lax.fori_loop(0, pieces, one, 0)

    def for_far(p, carry):
        own = term(far, p)
        sib_copy(0, p).wait_recv()
        to_far[p] = (own + from_sib[0, p].astype(jnp.float32)).astype(jnp.bfloat16)
        far_copy(p).start()
        return carry

    def for_out(p, carry):
        own = term(t, p)
        sib_copy(1, p).wait_recv()
        own = own + from_sib[1, p].astype(jnp.float32)
        far_copy(p).wait_recv()
        out_ref[:, pl.ds(pl.multiple_of(p * PIECE, PIECE), PIECE)] = (
            own + from_far[p].astype(jnp.float32)
        ).astype(jnp.bfloat16)
        return carry

    for_sib(0, (sib + 2) % 4)
    lax.fori_loop(0, pieces, for_far, 0)
    for_sib(1, sib)
    lax.fori_loop(0, pieces, for_out, 0)

    def drain(p, carry):
        sib_copy(0, p).wait_send()
        sib_copy(1, p).wait_send()
        far_copy(p).wait_send()
        return carry

    lax.fori_loop(0, pieces, drain, 0)

    def drain_ctx(j, carry):
        slab = c % 2 + 2 * j
        for h in range(heads):
            ctx_copy(h, slab, 2, c).wait_send()

            @pl.when((j <= z) & (z < depth - 1))
            def _():
                ctx_copy(h, slab, 0, c).wait_send()

            @pl.when((j >= z) & (z > 0))
            def _():
                ctx_copy(h, slab, 1, c).wait_send()

        return carry

    lax.fori_loop(0, depth, drain_ctx, 0)


def fused_device(
    n,
    queries,
    key_states,
    value_states,
    attn_output,
    output_grad,
    block_map,
    w_query,
    w_key,
    w_value,
):
    slab_rows, width = queries.shape
    heads = width // HD
    tokens = n * slab_rows
    model = w_query.shape[0]
    block_rows = tokens // 4
    pieces = model // PIECE
    vmem = pl.BlockSpec(memory_space=pltpu.VMEM)
    dma = pltpu.SemaphoreType.DMA
    return pl.pallas_call(
        functools.partial(fused_kernel, n),
        out_shape=jax.ShapeDtypeStruct((block_rows, model), jnp.bfloat16),
        in_specs=[vmem] * 5
        + [pl.BlockSpec(memory_space=pltpu.SMEM)]
        + [pl.BlockSpec(memory_space=pl.ANY)] * 3,
        out_specs=vmem,
        scratch_shapes=[
            pltpu.VMEM((heads, n, CHUNK, HD), jnp.bfloat16),
            pltpu.VMEM((n, tokens), jnp.float32),
            pltpu.VMEM((tokens, HD), jnp.float32),
            pltpu.VMEM((tokens, HD), jnp.float32),
            pltpu.VMEM((tokens, 3 * width), jnp.bfloat16),
            pltpu.VMEM((model, 3 * width), jnp.bfloat16),
            pltpu.VMEM((2, pieces, block_rows, PIECE), jnp.bfloat16),
            pltpu.VMEM((2, pieces, block_rows, PIECE), jnp.bfloat16),
            pltpu.VMEM((pieces, block_rows, PIECE), jnp.bfloat16),
            pltpu.VMEM((pieces, block_rows, PIECE), jnp.bfloat16),
            dma((3,)),
            dma((heads, 3, n)),
            dma((heads, n)),
            dma((2, pieces)),
            dma((2, pieces)),
            dma((pieces,)),
            dma((pieces,)),
        ],
        compiler_params=pltpu.CompilerParams(
            collective_id=0, has_side_effects=True, vmem_limit_bytes=48 * 1024 * 1024
        ),
        cost_estimate=pl.CostEstimate(
            flops=10 * heads * tokens * tokens * HD + 6 * tokens * model * width,
            bytes_accessed=6 * model * width + 2 * block_rows * model,
            transcendentals=heads * tokens * tokens,
        ),
    )(
        queries,
        key_states,
        value_states,
        attn_output,
        output_grad,
        block_map,
        w_query,
        w_key,
        w_value,
    )


def solution(mesh):
    context_count, group_count = mesh.shape["ctx"], mesh.shape["tp"]
    if context_count == 8 and group_count == 4:
        body = functools.partial(fused_device, context_count)
    else:
        body = per_device
    return jax.shard_map(
        body,
        mesh=mesh,
        in_specs=(
            P("ctx", "tp"),
            P("ctx", "tp"),
            P("ctx", "tp"),
            P("ctx", "tp"),
            P("ctx", "tp"),
            P(),
            P("ctx", "tp"),
            P("ctx", "tp"),
            P("ctx", "tp"),
        ),
        out_specs=P("tp", "ctx"),
        check_vma=False,
    )
```

```python
import functools
import math

import jax
import jax.numpy as jnp
from jax import lax
from jax.experimental import pallas as pl
from jax.experimental.pallas import tpu as pltpu
from jax.sharding import PartitionSpec as P

HD = 128
BLK = 128


NEG_FILL = -1e30


def block_mask(block_map, row_offset, row_count, col_offset, col_count):
    tiles = lax.dynamic_slice(
        block_map, (row_offset // BLK, col_offset // BLK), (row_count // BLK, col_count // BLK)
    )
    spread = jnp.broadcast_to(
        tiles[:, None, :, None], (row_count // BLK, BLK, col_count // BLK, BLK)
    )
    return spread.reshape(row_count, col_count) > 0


def resolved_rows(values):
    return lax.optimization_barrier(values.astype(jnp.bfloat16)).astype(jnp.float32)


def stat_update(state, query_heads, key_block, allowed, score_scale):
    row_max, row_sum = state
    scores = (
        jnp.einsum("qhd,khd->hqk", query_heads, key_block, preferred_element_type=jnp.float32)
        * score_scale
    )
    masked = jnp.where(allowed[None], scores, NEG_FILL)
    new_max = jnp.maximum(row_max, jnp.max(masked, axis=2))
    kept = jnp.where(allowed[None], jnp.exp(masked - new_max[:, :, None]), 0.0)
    return (new_max, row_sum * jnp.exp(row_max - new_max) + jnp.sum(kept, axis=2))


def gradient_block(
    query_heads, grad_heads, key_block, value_block, log_total, row_delta, allowed, score_scale
):
    scores = (
        jnp.einsum("qhd,khd->hqk", query_heads, key_block, preferred_element_type=jnp.float32)
        * score_scale
    )
    masked = jnp.where(allowed[None], scores, NEG_FILL)
    probs = jnp.where(allowed[None], jnp.exp(masked - log_total[:, :, None]), 0.0)
    probs_low = probs.astype(jnp.bfloat16)
    dprobs = jnp.einsum("qhd,khd->hqk", grad_heads, value_block, preferred_element_type=jnp.float32)
    score_gradient = (probs * (dprobs - row_delta[:, :, None]) * score_scale).astype(jnp.bfloat16)
    return (probs_low, score_gradient)


def per_device(
    queries, key_states, value_states, attn_output, output_grad, block_map, w_query, w_key, w_value
):
    slab_rows, width = queries.shape
    head_count = width // HD
    context_count = lax.axis_size("ctx")
    score_scale = 1.0 / math.sqrt(HD)
    row_offset = lax.axis_index("ctx") * slab_rows
    query_heads = queries.reshape(slab_rows, head_count, HD)
    grad_heads = output_grad.reshape(slab_rows, head_count, HD)
    output_heads = attn_output.reshape(slab_rows, head_count, HD)
    row_delta = jnp.sum(grad_heads.astype(jnp.float32) * output_heads.astype(jnp.float32), axis=2).T
    start_state = (
        jnp.full((head_count, slab_rows), NEG_FILL, jnp.float32),
        jnp.zeros((head_count, slab_rows), jnp.float32),
    )
    full_keys, full_values = (
        lax.all_gather(key_states, "ctx", axis=0, tiled=True),
        lax.all_gather(value_states, "ctx", axis=0, tiled=True),
    )
    group_size = min(context_count, max(1, 512 // slab_rows))
    key_span = slab_rows * group_size
    total_block_count = context_count // group_size
    key_blocks = full_keys.reshape(total_block_count, key_span, head_count, HD)
    value_blocks = full_values.reshape(total_block_count, key_span, head_count, HD)
    block_ids = jnp.arange(total_block_count, dtype=jnp.int32)

    def stat_step(state, inputs):
        key_block, block_index = inputs
        allowed = block_mask(block_map, row_offset, slab_rows, block_index * key_span, key_span)

        def stat_active_step(previous):
            return stat_update(previous, query_heads, key_block, allowed, score_scale)

        return (
            lax.cond(jnp.any(allowed), stat_active_step, lambda previous: previous, state),
            None,
        )

    (row_max, row_sum), _ = lax.scan(stat_step, start_state, (key_blocks, block_ids))
    log_total = row_max + jnp.log(row_sum)

    def back_step(dq_total, inputs):
        key_block, value_block, block_index = inputs
        allowed = block_mask(block_map, row_offset, slab_rows, block_index * key_span, key_span)

        def back_active_step(previous):
            probs_low, score_gradient = gradient_block(
                query_heads,
                grad_heads,
                key_block,
                value_block,
                log_total,
                row_delta,
                allowed,
                score_scale,
            )
            dv_part = jnp.einsum(
                "hqk,qhd->khd", probs_low, grad_heads, preferred_element_type=jnp.float32
            ).astype(jnp.bfloat16)
            dk_part = jnp.einsum(
                "hqk,qhd->khd", score_gradient, query_heads, preferred_element_type=jnp.float32
            ).astype(jnp.bfloat16)
            per_slab = jnp.einsum(
                "hqgk,gkhd->gqhd",
                score_gradient.reshape(head_count, slab_rows, group_size, slab_rows),
                key_block.reshape(group_size, slab_rows, head_count, HD),
                preferred_element_type=jnp.float32,
            )
            joined = jnp.concatenate(
                [dk_part.reshape(key_span, width), dv_part.reshape(key_span, width)], axis=1
            )
            return (previous + jnp.sum(resolved_rows(per_slab), axis=0), joined)

        def empty_step(previous):
            return (previous, jnp.zeros((key_span, 2 * width), jnp.bfloat16))

        return lax.cond(jnp.any(allowed), back_active_step, empty_step, dq_total)

    dq_total, joined_blocks = lax.scan(
        back_step,
        jnp.zeros((slab_rows, head_count, HD), jnp.float32),
        (key_blocks, value_blocks, block_ids),
    )
    local_grads = dq_total.astype(jnp.bfloat16).reshape(slab_rows, width)
    part_grads = joined_blocks.reshape(context_count * slab_rows, 2 * width)
    part_width = part_grads.shape[1]
    arrived = lax.all_to_all(
        part_grads.reshape(context_count, slab_rows, part_width),
        "ctx",
        split_axis=0,
        concat_axis=0,
        tiled=True,
    )
    finished = jnp.sum(arrived.astype(jnp.float32), axis=0).astype(jnp.bfloat16)
    own_grads = jnp.concatenate([local_grads, finished], axis=1)
    gradients = lax.all_gather(own_grads, "ctx", axis=0, tiled=True)
    projections = jnp.concatenate([w_query, w_key, w_value], axis=1)
    return lax.psum_scatter(
        lax.dot_general(
            gradients, projections, (((1,), (1,)), ((), ())), preferred_element_type=jnp.float32
        ).astype(jnp.bfloat16),
        "tp",
        scatter_dimension=0,
        tiled=True,
    )


MESH = pl.DeviceIdType.MESH
LOG2E = 1.4426950408889634
PAIR = 2 * BLK
TAIL = 16
PIECE = 256


def contract(a, b, da, db):
    return lax.dot_general(a, b, (((da,), (db,)), ((), ())), preferred_element_type=jnp.float32)


def fused_kernel(
    n,
    q_hbm,
    k_hbm,
    v_hbm,
    o_hbm,
    g_hbm,
    map_ref,
    wq_hbm,
    wk_hbm,
    wv_hbm,
    out_ref,
    held_qk,
    held_g,
    held_v,
    o_ref,
    bias,
    probs_ref,
    delta_ref,
    dq_acc,
    grads,
    w_ref,
    to_sib,
    from_sib,
    to_far,
    from_far,
    w_sem,
    in_sem,
    ctx_send,
    ctx_recv,
    sib_send,
    sib_recv,
    far_send,
    far_recv,
):
    heads = held_qk.shape[0]
    depth = n // 2
    tokens = n * BLK
    pieces = to_far.shape[0]
    block_rows = to_far.shape[1]
    c = lax.axis_index("ctx")
    t = lax.axis_index("tp")
    z = c // 2
    other = c + 1 - 2 * (c % 2)
    sib = t + 1 - 2 * (t % 2)
    far = (t + 2) % 4
    scale = 1.0 / math.sqrt(HD)

    barrier = pltpu.get_barrier_semaphore()
    for peer in ({"ctx": other}, {"tp": sib}, {"tp": far}):
        pl.semaphore_signal(barrier, inc=1, device_id=peer, device_id_type=MESH)

    @pl.when(z > 0)
    def _():
        pl.semaphore_signal(barrier, inc=1, device_id={"ctx": c - 2}, device_id_type=MESH)

    @pl.when(z < depth - 1)
    def _():
        pl.semaphore_signal(barrier, inc=1, device_id={"ctx": c + 2}, device_id_type=MESH)

    in_copies = [pltpu.make_async_copy(o_hbm, o_ref, in_sem.at[4 * heads])]
    for h in range(heads):
        cols = pl.ds(h * HD, HD)
        for i, (source, target) in enumerate(
            (
                (q_hbm, held_qk.at[h, c, pl.ds(0, BLK)]),
                (k_hbm, held_qk.at[h, c, pl.ds(BLK, BLK)]),
                (g_hbm, held_g.at[h, c, pl.ds(0, BLK)]),
                (v_hbm, held_v.at[h, c]),
            )
        ):
            in_copies.append(
                pltpu.make_async_copy(source.at[:, cols], target, in_sem.at[4 * h + i])
            )
    for copy in in_copies:
        copy.start()
    w_copies = [
        pltpu.make_async_copy(w, w_ref.at[:, pl.ds(i * heads * HD, heads * HD)], w_sem.at[i])
        for i, w in enumerate((wq_hbm, wk_hbm, wv_hbm))
    ]
    for copy in w_copies:
        copy.start()
    for copy in in_copies:
        copy.wait()

    for h in range(heads):
        grad = held_g[h, c, 0:BLK, :].astype(jnp.float32)
        product = grad * o_ref[:, h * HD : (h + 1) * HD].astype(jnp.float32)
        delta = jnp.sum(product.T, axis=0, keepdims=True)
        high = delta.astype(jnp.bfloat16)
        rest = delta - high.astype(jnp.float32)
        middle = rest.astype(jnp.bfloat16)
        low = (rest - middle.astype(jnp.float32)).astype(jnp.bfloat16)
        held_g[h, c, BLK : BLK + TAIL, :] = jnp.concatenate(
            [high, middle, low, jnp.zeros((TAIL - 3, BLK), jnp.bfloat16)], axis=0
        )

    stores = (held_qk, held_g, held_v)
    streams = [(kind, h) for kind in range(3) for h in range(heads)]

    def ctx_copy(s, slab, way, target):
        kind, h = streams[s]
        return pltpu.make_async_remote_copy(
            src_ref=stores[kind].at[h, slab],
            dst_ref=stores[kind].at[h, slab],
            send_sem=ctx_send.at[s, way, slab],
            recv_sem=ctx_recv.at[s, slab],
            device_id={"ctx": target},
            device_id_type=MESH,
        )

    def send_up(h, slab):
        @pl.when(z < depth - 1)
        def _():
            ctx_copy(h, slab, 0, c + 2).start()

    def send_down(h, slab):
        @pl.when(z > 0)
        def _():
            ctx_copy(h, slab, 1, c - 2).start()

    def send_own(h):
        send_up(h, c)
        send_down(h, c)
        ctx_copy(h, c, 2, other).start()

    def pass_on(h, d):
        @pl.when(z - d >= 0)
        def _():
            slab = c - 2 * d
            ctx_copy(h, slab, 0, c).wait_recv()
            send_up(h, slab)
            ctx_copy(h, slab, 2, other).start()

        @pl.when(z + d < depth)
        def _():
            slab = c + 2 * d
            ctx_copy(h, slab, 0, c).wait_recv()
            send_down(h, slab)
            ctx_copy(h, slab, 2, other).start()

    pl.semaphore_wait(
        barrier,
        3 + jnp.where(z > 0, 1, 0) + jnp.where(z < depth - 1, 1, 0),
    )
    send_own(0)
    send_own(1)

    for a in range(n):
        for b in range(n):
            bias[b : b + 1, a * BLK : (a + 1) * BLK] = jnp.full(
                (1, BLK), jnp.where(map_ref[a, b] > 0, 0.0, NEG_FILL), jnp.float32
            )
    dq_acc[...] = jnp.zeros_like(dq_acc)

    def soften(h, i):
        keys = held_qk[h, :, BLK : 2 * BLK, :].reshape(tokens, HD)
        pair_q = held_qk[h, pl.ds(2 * i, 2), 0:BLK, :].reshape(PAIR, HD)
        columns = pl.ds(pl.multiple_of(i * PAIR, PAIR), PAIR)
        scores = contract(keys, pair_q, 1, 1) * (scale * LOG2E)
        masked = scores.reshape(n, BLK, PAIR) + bias[:, columns][:, None, :]
        top = jnp.max(masked, axis=(0, 1), keepdims=True)
        raised = jnp.exp2(masked - top)
        total = jnp.sum(raised, axis=(0, 1), keepdims=True)
        probs = (raised * (1.0 / total)).reshape(tokens, PAIR)
        probs_ref[h, :, columns] = probs.astype(jnp.bfloat16)

    def value_rows(h, i):
        rows = pl.ds(pl.multiple_of(i * PAIR, PAIR), PAIR)
        all_g = held_g[h, :, 0:BLK, :].reshape(tokens, HD)
        first = (2 * heads + h) * HD
        grads[rows, first : first + HD] = contract(probs_ref[h, rows, :], all_g, 1, 0).astype(
            jnp.bfloat16
        )

    def key_rows(h, i):
        rows = pl.ds(pl.multiple_of(i * PAIR, PAIR), PAIR)
        pair = pl.ds(2 * i, 2)
        all_g = held_g[h, :, 0:BLK, :].reshape(tokens, HD)
        all_q = held_qk[h, :, 0:BLK, :].reshape(tokens, HD)
        keys = held_qk[h, pair, BLK : 2 * BLK, :].reshape(PAIR, HD)
        values = held_v[h, pair, :, :].reshape(PAIR, HD)
        dprobs = contract(values, all_g, 1, 1)
        probs = probs_ref[h, rows, :].astype(jnp.float32)
        dscores = (probs * (dprobs - delta_ref[h : h + 1, :])).astype(jnp.bfloat16)
        first = (heads + h) * HD
        grads[rows, first : first + HD] = (contract(dscores, all_q, 1, 0) * scale).astype(
            jnp.bfloat16
        )
        dq_acc[h] += contract(keys, dscores, 0, 0)

    def spread_delta(h):
        sums = jnp.sum(held_g[h, :, BLK : BLK + TAIL, :].astype(jnp.float32), axis=1)
        for a in range(n):
            delta_ref[h : h + 1, a * BLK : (a + 1) * BLK] = sums[a : a + 1]

    def passive(s):
        def one(j, carry):
            ctx_copy(s, (1 - c % 2) + 2 * j, 0, c).wait_recv()
            return carry

        lax.fori_loop(0, depth, one, 0)

    last = len(streams) - 1
    for d in range(1, depth):
        pass_on(0, d)
    for s, (kind, h) in enumerate(streams):
        passive(s)
        if s + 2 <= last:
            send_own(s + 2)
        if kind == 1:
            spread_delta(h)
        work = (soften, value_rows, key_rows)[kind]

        def step(i, carry, s=s, h=h, work=work):
            if s < last:

                @pl.when(i >= 1)
                def _():
                    pass_on(s + 1, i)

            work(h, i)
            return carry

        lax.fori_loop(0, depth, step, 0)
        if kind == 2:
            grads[:, h * HD : (h + 1) * HD] = (dq_acc[h].T * scale).astype(jnp.bfloat16)
    for copy in w_copies:
        copy.wait()

    def term(block, p):
        rows = grads[pl.ds(pl.multiple_of(block * block_rows, block_rows), block_rows), :]
        return contract(rows, w_ref[pl.ds(pl.multiple_of(p * PIECE, PIECE), PIECE), :], 1, 1)

    def sib_copy(k, p):
        return pltpu.make_async_remote_copy(
            src_ref=to_sib.at[k, p],
            dst_ref=from_sib.at[k, p],
            send_sem=sib_send.at[k, p],
            recv_sem=sib_recv.at[k, p],
            device_id={"tp": sib},
            device_id_type=MESH,
        )

    def far_copy(p):
        return pltpu.make_async_remote_copy(
            src_ref=to_far.at[p],
            dst_ref=from_far.at[p],
            send_sem=far_send.at[p],
            recv_sem=far_recv.at[p],
            device_id={"tp": far},
            device_id_type=MESH,
        )

    def for_sib(k, block):
        def one(p, carry):
            to_sib[k, p] = term(block, p).astype(jnp.bfloat16)
            sib_copy(k, p).start()
            return carry

        lax.fori_loop(0, pieces, one, 0)

    def for_far(p, carry):
        own = term(far, p)
        sib_copy(0, p).wait_recv()
        to_far[p] = (own + from_sib[0, p].astype(jnp.float32)).astype(jnp.bfloat16)
        far_copy(p).start()
        return carry

    def for_out(p, carry):
        own = term(t, p)
        sib_copy(1, p).wait_recv()
        own = own + from_sib[1, p].astype(jnp.float32)
        far_copy(p).wait_recv()
        out_ref[:, pl.ds(pl.multiple_of(p * PIECE, PIECE), PIECE)] = (
            own + from_far[p].astype(jnp.float32)
        ).astype(jnp.bfloat16)
        return carry

    for_sib(0, (sib + 2) % 4)
    lax.fori_loop(0, pieces, for_far, 0)
    for_sib(1, sib)
    lax.fori_loop(0, pieces, for_out, 0)

    def drain(p, carry):
        sib_copy(0, p).wait_send()
        sib_copy(1, p).wait_send()
        far_copy(p).wait_send()
        return carry

    lax.fori_loop(0, pieces, drain, 0)

    def drain_ctx(j, carry):
        slab = c % 2 + 2 * j
        for h in range(len(streams)):
            ctx_copy(h, slab, 2, c).wait_send()

            @pl.when((j <= z) & (z < depth - 1))
            def _():
                ctx_copy(h, slab, 0, c).wait_send()

            @pl.when((j >= z) & (z > 0))
            def _():
                ctx_copy(h, slab, 1, c).wait_send()

        return carry

    lax.fori_loop(0, depth, drain_ctx, 0)


def fused_device(
    n,
    queries,
    key_states,
    value_states,
    attn_output,
    output_grad,
    block_map,
    w_query,
    w_key,
    w_value,
):
    slab_rows, width = queries.shape
    heads = width // HD
    tokens = n * slab_rows
    model = w_query.shape[0]
    block_rows = tokens // 4
    pieces = model // PIECE
    vmem = pl.BlockSpec(memory_space=pltpu.VMEM)
    dma = pltpu.SemaphoreType.DMA
    return pl.pallas_call(
        functools.partial(fused_kernel, n),
        out_shape=jax.ShapeDtypeStruct((block_rows, model), jnp.bfloat16),
        in_specs=[pl.BlockSpec(memory_space=pl.ANY)] * 5
        + [pl.BlockSpec(memory_space=pltpu.SMEM)]
        + [pl.BlockSpec(memory_space=pl.ANY)] * 3,
        out_specs=vmem,
        scratch_shapes=[
            pltpu.VMEM((heads, n, 2 * BLK, HD), jnp.bfloat16),
            pltpu.VMEM((heads, n, BLK + TAIL, HD), jnp.bfloat16),
            pltpu.VMEM((heads, n, BLK, HD), jnp.bfloat16),
            pltpu.VMEM((slab_rows, width), jnp.bfloat16),
            pltpu.VMEM((n, tokens), jnp.float32),
            pltpu.VMEM((heads, tokens, tokens), jnp.bfloat16),
            pltpu.VMEM((heads, tokens), jnp.float32),
            pltpu.VMEM((heads, HD, tokens), jnp.float32),
            pltpu.VMEM((tokens, 3 * width), jnp.bfloat16),
            pltpu.VMEM((model, 3 * width), jnp.bfloat16),
            pltpu.VMEM((2, pieces, block_rows, PIECE), jnp.bfloat16),
            pltpu.VMEM((2, pieces, block_rows, PIECE), jnp.bfloat16),
            pltpu.VMEM((pieces, block_rows, PIECE), jnp.bfloat16),
            pltpu.VMEM((pieces, block_rows, PIECE), jnp.bfloat16),
            dma((3,)),
            dma((4 * heads + 1,)),
            dma((3 * heads, 3, n)),
            dma((3 * heads, n)),
            dma((2, pieces)),
            dma((2, pieces)),
            dma((pieces,)),
            dma((pieces,)),
        ],
        compiler_params=pltpu.CompilerParams(
            collective_id=0, has_side_effects=True, vmem_limit_bytes=62 * 1024 * 1024
        ),
        cost_estimate=pl.CostEstimate(
            flops=10 * heads * tokens * tokens * HD + 6 * tokens * model * width,
            bytes_accessed=6 * model * width + 2 * block_rows * model,
            transcendentals=heads * tokens * tokens,
        ),
    )(
        queries,
        key_states,
        value_states,
        attn_output,
        output_grad,
        block_map,
        w_query,
        w_key,
        w_value,
    )


def solution(mesh):
    context_count, group_count = mesh.shape["ctx"], mesh.shape["tp"]
    if context_count == 8 and group_count == 4:
        body = functools.partial(fused_device, context_count)
    else:
        body = per_device
    return jax.shard_map(
        body,
        mesh=mesh,
        in_specs=(
            P("ctx", "tp"),
            P("ctx", "tp"),
            P("ctx", "tp"),
            P("ctx", "tp"),
            P("ctx", "tp"),
            P(),
            P("ctx", "tp"),
            P("ctx", "tp"),
            P("ctx", "tp"),
        ),
        out_specs=P("tp", "ctx"),
        check_vma=False,
    )
```

```python
import functools
import math

import jax
import jax.numpy as jnp
from jax import lax
from jax.experimental import pallas as pl
from jax.experimental.pallas import tpu as pltpu
from jax.sharding import PartitionSpec as P

HD = 128
BLK = 128


NEG_FILL = -1e30


def block_mask(block_map, row_offset, row_count, col_offset, col_count):
    tiles = lax.dynamic_slice(
        block_map, (row_offset // BLK, col_offset // BLK), (row_count // BLK, col_count // BLK)
    )
    spread = jnp.broadcast_to(
        tiles[:, None, :, None], (row_count // BLK, BLK, col_count // BLK, BLK)
    )
    return spread.reshape(row_count, col_count) > 0


def resolved_rows(values):
    return lax.optimization_barrier(values.astype(jnp.bfloat16)).astype(jnp.float32)


def stat_update(state, query_heads, key_block, allowed, score_scale):
    row_max, row_sum = state
    scores = (
        jnp.einsum("qhd,khd->hqk", query_heads, key_block, preferred_element_type=jnp.float32)
        * score_scale
    )
    masked = jnp.where(allowed[None], scores, NEG_FILL)
    new_max = jnp.maximum(row_max, jnp.max(masked, axis=2))
    kept = jnp.where(allowed[None], jnp.exp(masked - new_max[:, :, None]), 0.0)
    return (new_max, row_sum * jnp.exp(row_max - new_max) + jnp.sum(kept, axis=2))


def gradient_block(
    query_heads, grad_heads, key_block, value_block, log_total, row_delta, allowed, score_scale
):
    scores = (
        jnp.einsum("qhd,khd->hqk", query_heads, key_block, preferred_element_type=jnp.float32)
        * score_scale
    )
    masked = jnp.where(allowed[None], scores, NEG_FILL)
    probs = jnp.where(allowed[None], jnp.exp(masked - log_total[:, :, None]), 0.0)
    probs_low = probs.astype(jnp.bfloat16)
    dprobs = jnp.einsum("qhd,khd->hqk", grad_heads, value_block, preferred_element_type=jnp.float32)
    score_gradient = (probs * (dprobs - row_delta[:, :, None]) * score_scale).astype(jnp.bfloat16)
    return (probs_low, score_gradient)


def per_device(
    queries, key_states, value_states, attn_output, output_grad, block_map, w_query, w_key, w_value
):
    slab_rows, width = queries.shape
    head_count = width // HD
    context_count = lax.axis_size("ctx")
    score_scale = 1.0 / math.sqrt(HD)
    row_offset = lax.axis_index("ctx") * slab_rows
    query_heads = queries.reshape(slab_rows, head_count, HD)
    grad_heads = output_grad.reshape(slab_rows, head_count, HD)
    output_heads = attn_output.reshape(slab_rows, head_count, HD)
    row_delta = jnp.sum(grad_heads.astype(jnp.float32) * output_heads.astype(jnp.float32), axis=2).T
    start_state = (
        jnp.full((head_count, slab_rows), NEG_FILL, jnp.float32),
        jnp.zeros((head_count, slab_rows), jnp.float32),
    )
    full_keys, full_values = (
        lax.all_gather(key_states, "ctx", axis=0, tiled=True),
        lax.all_gather(value_states, "ctx", axis=0, tiled=True),
    )
    group_size = min(context_count, max(1, 512 // slab_rows))
    key_span = slab_rows * group_size
    total_block_count = context_count // group_size
    key_blocks = full_keys.reshape(total_block_count, key_span, head_count, HD)
    value_blocks = full_values.reshape(total_block_count, key_span, head_count, HD)
    block_ids = jnp.arange(total_block_count, dtype=jnp.int32)

    def stat_step(state, inputs):
        key_block, block_index = inputs
        allowed = block_mask(block_map, row_offset, slab_rows, block_index * key_span, key_span)

        def stat_active_step(previous):
            return stat_update(previous, query_heads, key_block, allowed, score_scale)

        return (
            lax.cond(jnp.any(allowed), stat_active_step, lambda previous: previous, state),
            None,
        )

    (row_max, row_sum), _ = lax.scan(stat_step, start_state, (key_blocks, block_ids))
    log_total = row_max + jnp.log(row_sum)

    def back_step(dq_total, inputs):
        key_block, value_block, block_index = inputs
        allowed = block_mask(block_map, row_offset, slab_rows, block_index * key_span, key_span)

        def back_active_step(previous):
            probs_low, score_gradient = gradient_block(
                query_heads,
                grad_heads,
                key_block,
                value_block,
                log_total,
                row_delta,
                allowed,
                score_scale,
            )
            dv_part = jnp.einsum(
                "hqk,qhd->khd", probs_low, grad_heads, preferred_element_type=jnp.float32
            ).astype(jnp.bfloat16)
            dk_part = jnp.einsum(
                "hqk,qhd->khd", score_gradient, query_heads, preferred_element_type=jnp.float32
            ).astype(jnp.bfloat16)
            per_slab = jnp.einsum(
                "hqgk,gkhd->gqhd",
                score_gradient.reshape(head_count, slab_rows, group_size, slab_rows),
                key_block.reshape(group_size, slab_rows, head_count, HD),
                preferred_element_type=jnp.float32,
            )
            joined = jnp.concatenate(
                [dk_part.reshape(key_span, width), dv_part.reshape(key_span, width)], axis=1
            )
            return (previous + jnp.sum(resolved_rows(per_slab), axis=0), joined)

        def empty_step(previous):
            return (previous, jnp.zeros((key_span, 2 * width), jnp.bfloat16))

        return lax.cond(jnp.any(allowed), back_active_step, empty_step, dq_total)

    dq_total, joined_blocks = lax.scan(
        back_step,
        jnp.zeros((slab_rows, head_count, HD), jnp.float32),
        (key_blocks, value_blocks, block_ids),
    )
    local_grads = dq_total.astype(jnp.bfloat16).reshape(slab_rows, width)
    part_grads = joined_blocks.reshape(context_count * slab_rows, 2 * width)
    part_width = part_grads.shape[1]
    arrived = lax.all_to_all(
        part_grads.reshape(context_count, slab_rows, part_width),
        "ctx",
        split_axis=0,
        concat_axis=0,
        tiled=True,
    )
    finished = jnp.sum(arrived.astype(jnp.float32), axis=0).astype(jnp.bfloat16)
    own_grads = jnp.concatenate([local_grads, finished], axis=1)
    gradients = lax.all_gather(own_grads, "ctx", axis=0, tiled=True)
    projections = jnp.concatenate([w_query, w_key, w_value], axis=1)
    return lax.psum_scatter(
        lax.dot_general(
            gradients, projections, (((1,), (1,)), ((), ())), preferred_element_type=jnp.float32
        ).astype(jnp.bfloat16),
        "tp",
        scatter_dimension=0,
        tiled=True,
    )


MESH = pl.DeviceIdType.MESH
LOG2E = 1.4426950408889634
PAIR = 2 * BLK
TAIL = 16
PIECE = 256


def contract(a, b, da, db):
    return lax.dot_general(a, b, (((da,), (db,)), ((), ())), preferred_element_type=jnp.float32)


def fused_kernel(
    n,
    q_hbm,
    k_hbm,
    v_hbm,
    o_hbm,
    g_hbm,
    map_ref,
    wq_hbm,
    wk_hbm,
    wv_hbm,
    out_ref,
    held_qk,
    held_g,
    o_ref,
    bias,
    probs_ref,
    delta_ref,
    dq_acc,
    grads,
    w_ref,
    to_sib,
    from_sib,
    to_far,
    from_far,
    w_sem,
    in_sem,
    ctx_send,
    ctx_recv,
    sib_send,
    sib_recv,
    far_send,
    far_recv,
):
    heads = held_qk.shape[0]
    depth = n // 2
    tokens = n * BLK
    pieces = to_far.shape[0]
    block_rows = to_far.shape[1]
    c = lax.axis_index("ctx")
    t = lax.axis_index("tp")
    z = c // 2
    other = c + 1 - 2 * (c % 2)
    sib = t + 1 - 2 * (t % 2)
    far = (t + 2) % 4
    scale = 1.0 / math.sqrt(HD)

    barrier = pltpu.get_barrier_semaphore()
    for peer in ({"ctx": other}, {"tp": sib}, {"tp": far}):
        pl.semaphore_signal(barrier, inc=1, device_id=peer, device_id_type=MESH)

    @pl.when(z > 0)
    def _():
        pl.semaphore_signal(barrier, inc=1, device_id={"ctx": c - 2}, device_id_type=MESH)

    @pl.when(z < depth - 1)
    def _():
        pl.semaphore_signal(barrier, inc=1, device_id={"ctx": c + 2}, device_id_type=MESH)

    in_copies = [pltpu.make_async_copy(o_hbm, o_ref, in_sem.at[4 * heads])]
    for h in range(heads):
        cols = pl.ds(h * HD, HD)
        for i, (source, target) in enumerate(
            (
                (q_hbm, held_qk.at[h, c, pl.ds(0, BLK)]),
                (k_hbm, held_qk.at[h, c, pl.ds(BLK, BLK)]),
                (g_hbm, held_g.at[h, c, pl.ds(0, BLK)]),
                (v_hbm, held_g.at[h, c, pl.ds(BLK, BLK)]),
            )
        ):
            in_copies.append(
                pltpu.make_async_copy(source.at[:, cols], target, in_sem.at[4 * h + i])
            )
    for copy in in_copies:
        copy.start()
    w_copies = [
        pltpu.make_async_copy(w, w_ref.at[:, pl.ds(i * heads * HD, heads * HD)], w_sem.at[i])
        for i, w in enumerate((wq_hbm, wk_hbm, wv_hbm))
    ]
    for copy in w_copies:
        copy.start()
    for copy in in_copies:
        copy.wait()

    for h in range(heads):
        grad = held_g[h, c, 0:BLK, :].astype(jnp.float32)
        product = grad * o_ref[:, h * HD : (h + 1) * HD].astype(jnp.float32)
        delta = jnp.sum(product.T, axis=0, keepdims=True)
        high = delta.astype(jnp.bfloat16)
        rest = delta - high.astype(jnp.float32)
        middle = rest.astype(jnp.bfloat16)
        low = (rest - middle.astype(jnp.float32)).astype(jnp.bfloat16)
        held_g[h, c, 2 * BLK : 2 * BLK + TAIL, :] = jnp.concatenate(
            [high, middle, low, jnp.zeros((TAIL - 3, BLK), jnp.bfloat16)], axis=0
        )

    stores = (held_qk, held_g)
    streams = [(kind, h) for kind in range(2) for h in range(heads)]

    def ctx_copy(s, slab, way, target):
        kind, h = streams[s]
        return pltpu.make_async_remote_copy(
            src_ref=stores[kind].at[h, slab],
            dst_ref=stores[kind].at[h, slab],
            send_sem=ctx_send.at[s, way, slab],
            recv_sem=ctx_recv.at[s, slab],
            device_id={"ctx": target},
            device_id_type=MESH,
        )

    def send_up(h, slab):
        @pl.when(z < depth - 1)
        def _():
            ctx_copy(h, slab, 0, c + 2).start()

    def send_down(h, slab):
        @pl.when(z > 0)
        def _():
            ctx_copy(h, slab, 1, c - 2).start()

    def send_own(h):
        send_up(h, c)
        send_down(h, c)
        ctx_copy(h, c, 2, other).start()

    def pass_on(h, d):
        @pl.when(z - d >= 0)
        def _():
            slab = c - 2 * d
            ctx_copy(h, slab, 0, c).wait_recv()
            send_up(h, slab)
            ctx_copy(h, slab, 2, other).start()

        @pl.when(z + d < depth)
        def _():
            slab = c + 2 * d
            ctx_copy(h, slab, 0, c).wait_recv()
            send_down(h, slab)
            ctx_copy(h, slab, 2, other).start()

    pl.semaphore_wait(
        barrier,
        3 + jnp.where(z > 0, 1, 0) + jnp.where(z < depth - 1, 1, 0),
    )
    for s in range(2):
        send_own(s)

    for a in range(n):
        for b in range(n):
            bias[b : b + 1, a * BLK : (a + 1) * BLK] = jnp.full(
                (1, BLK), jnp.where(map_ref[a, b] > 0, 0.0, NEG_FILL), jnp.float32
            )
    dq_acc[...] = jnp.zeros_like(dq_acc)

    def soften(h, i):
        keys = held_qk[h, :, BLK : 2 * BLK, :].reshape(tokens, HD)
        pair_q = held_qk[h, pl.ds(2 * i, 2), 0:BLK, :].reshape(PAIR, HD)
        columns = pl.ds(pl.multiple_of(i * PAIR, PAIR), PAIR)
        scores = contract(keys, pair_q, 1, 1) * (scale * LOG2E)
        masked = scores.reshape(n, BLK, PAIR) + bias[:, columns][:, None, :]
        top = jnp.max(masked, axis=(0, 1), keepdims=True)
        raised = jnp.exp2(masked - top)
        total = jnp.sum(raised, axis=(0, 1), keepdims=True)
        probs = (raised * (1.0 / total)).reshape(tokens, PAIR)
        probs_ref[h, :, columns] = probs.astype(jnp.bfloat16)

    def value_rows(h, i):
        rows = pl.ds(pl.multiple_of(i * PAIR, PAIR), PAIR)
        all_g = held_g[h, :, 0:BLK, :].reshape(tokens, HD)
        first = (2 * heads + h) * HD
        grads[rows, first : first + HD] = contract(probs_ref[h, rows, :], all_g, 1, 0).astype(
            jnp.bfloat16
        )

    def key_rows(h, i):
        rows = pl.ds(pl.multiple_of(i * PAIR, PAIR), PAIR)
        pair = pl.ds(2 * i, 2)
        all_g = held_g[h, :, 0:BLK, :].reshape(tokens, HD)
        all_q = held_qk[h, :, 0:BLK, :].reshape(tokens, HD)
        keys = held_qk[h, pair, BLK : 2 * BLK, :].reshape(PAIR, HD)
        values = held_g[h, pair, BLK : 2 * BLK, :].reshape(PAIR, HD)
        dprobs = contract(values, all_g, 1, 1)
        probs = probs_ref[h, rows, :].astype(jnp.float32)
        dscores = (probs * (dprobs - delta_ref[h : h + 1, :])).astype(jnp.bfloat16)
        first = (heads + h) * HD
        grads[rows, first : first + HD] = (contract(dscores, all_q, 1, 0) * scale).astype(
            jnp.bfloat16
        )
        dq_acc[h] += contract(keys, dscores, 0, 0)

    def spread_delta(h):
        sums = jnp.sum(held_g[h, :, 2 * BLK : 2 * BLK + TAIL, :].astype(jnp.float32), axis=1)
        for a in range(n):
            delta_ref[h : h + 1, a * BLK : (a + 1) * BLK] = sums[a : a + 1]

    def passive(s):
        def one(j, carry):
            ctx_copy(s, (1 - c % 2) + 2 * j, 0, c).wait_recv()
            return carry

        lax.fori_loop(0, depth, one, 0)

    def backward(h, i):
        value_rows(h, i)
        key_rows(h, i)

    count = len(streams)
    for wave in range(1, count + depth):
        for d in range(depth - 1, 0, -1):
            if 0 <= wave - d < count:
                pass_on(wave - d, d)
        if wave + 1 < count:
            send_own(wave + 1)
        if wave < depth:
            continue
        s = wave - depth
        kind, h = streams[s]
        passive(s)
        if kind == 1:
            spread_delta(h)
        work = (soften, backward)[kind]

        def step(i, carry, h=h, work=work):
            work(h, i)
            return carry

        lax.fori_loop(0, depth, step, 0)
        if kind == 1:
            grads[:, h * HD : (h + 1) * HD] = (dq_acc[h].T * scale).astype(jnp.bfloat16)
    for copy in w_copies:
        copy.wait()

    def term(block, p):
        rows = grads[pl.ds(pl.multiple_of(block * block_rows, block_rows), block_rows), :]
        return contract(rows, w_ref[pl.ds(pl.multiple_of(p * PIECE, PIECE), PIECE), :], 1, 1)

    def sib_copy(k, p):
        return pltpu.make_async_remote_copy(
            src_ref=to_sib.at[k, p],
            dst_ref=from_sib.at[k, p],
            send_sem=sib_send.at[k, p],
            recv_sem=sib_recv.at[k, p],
            device_id={"tp": sib},
            device_id_type=MESH,
        )

    def far_copy(p):
        return pltpu.make_async_remote_copy(
            src_ref=to_far.at[p],
            dst_ref=from_far.at[p],
            send_sem=far_send.at[p],
            recv_sem=far_recv.at[p],
            device_id={"tp": far},
            device_id_type=MESH,
        )

    def for_sib(k, block):
        def one(p, carry):
            to_sib[k, p] = term(block, p).astype(jnp.bfloat16)
            sib_copy(k, p).start()
            return carry

        lax.fori_loop(0, pieces, one, 0)

    def for_far(p, carry):
        own = term(far, p)
        sib_copy(0, p).wait_recv()
        to_far[p] = (own + from_sib[0, p].astype(jnp.float32)).astype(jnp.bfloat16)
        far_copy(p).start()
        return carry

    def for_out(p, carry):
        own = term(t, p)
        sib_copy(1, p).wait_recv()
        own = own + from_sib[1, p].astype(jnp.float32)
        far_copy(p).wait_recv()
        out_ref[:, pl.ds(pl.multiple_of(p * PIECE, PIECE), PIECE)] = (
            own + from_far[p].astype(jnp.float32)
        ).astype(jnp.bfloat16)
        return carry

    for_sib(0, (sib + 2) % 4)
    lax.fori_loop(0, pieces, for_far, 0)
    for_sib(1, sib)
    lax.fori_loop(0, pieces, for_out, 0)

    def drain(p, carry):
        sib_copy(0, p).wait_send()
        sib_copy(1, p).wait_send()
        far_copy(p).wait_send()
        return carry

    lax.fori_loop(0, pieces, drain, 0)

    def drain_ctx(j, carry):
        slab = c % 2 + 2 * j
        for h in range(len(streams)):
            ctx_copy(h, slab, 2, c).wait_send()

            @pl.when((j <= z) & (z < depth - 1))
            def _():
                ctx_copy(h, slab, 0, c).wait_send()

            @pl.when((j >= z) & (z > 0))
            def _():
                ctx_copy(h, slab, 1, c).wait_send()

        return carry

    lax.fori_loop(0, depth, drain_ctx, 0)


def fused_device(
    n,
    queries,
    key_states,
    value_states,
    attn_output,
    output_grad,
    block_map,
    w_query,
    w_key,
    w_value,
):
    slab_rows, width = queries.shape
    heads = width // HD
    tokens = n * slab_rows
    model = w_query.shape[0]
    block_rows = tokens // 4
    pieces = model // PIECE
    vmem = pl.BlockSpec(memory_space=pltpu.VMEM)
    dma = pltpu.SemaphoreType.DMA
    return pl.pallas_call(
        functools.partial(fused_kernel, n),
        out_shape=jax.ShapeDtypeStruct((block_rows, model), jnp.bfloat16),
        in_specs=[pl.BlockSpec(memory_space=pl.ANY)] * 5
        + [pl.BlockSpec(memory_space=pltpu.SMEM)]
        + [pl.BlockSpec(memory_space=pl.ANY)] * 3,
        out_specs=vmem,
        scratch_shapes=[
            pltpu.VMEM((heads, n, 2 * BLK, HD), jnp.bfloat16),
            pltpu.VMEM((heads, n, 2 * BLK + TAIL, HD), jnp.bfloat16),
            pltpu.VMEM((slab_rows, width), jnp.bfloat16),
            pltpu.VMEM((n, tokens), jnp.float32),
            pltpu.VMEM((heads, tokens, tokens), jnp.bfloat16),
            pltpu.VMEM((heads, tokens), jnp.float32),
            pltpu.VMEM((heads, HD, tokens), jnp.float32),
            pltpu.VMEM((tokens, 3 * width), jnp.bfloat16),
            pltpu.VMEM((model, 3 * width), jnp.bfloat16),
            pltpu.VMEM((2, pieces, block_rows, PIECE), jnp.bfloat16),
            pltpu.VMEM((2, pieces, block_rows, PIECE), jnp.bfloat16),
            pltpu.VMEM((pieces, block_rows, PIECE), jnp.bfloat16),
            pltpu.VMEM((pieces, block_rows, PIECE), jnp.bfloat16),
            dma((3,)),
            dma((4 * heads + 1,)),
            dma((2 * heads, 3, n)),
            dma((2 * heads, n)),
            dma((2, pieces)),
            dma((2, pieces)),
            dma((pieces,)),
            dma((pieces,)),
        ],
        compiler_params=pltpu.CompilerParams(
            collective_id=0, has_side_effects=True, vmem_limit_bytes=62 * 1024 * 1024
        ),
        cost_estimate=pl.CostEstimate(
            flops=10 * heads * tokens * tokens * HD + 6 * tokens * model * width,
            bytes_accessed=6 * model * width + 2 * block_rows * model,
            transcendentals=heads * tokens * tokens,
        ),
    )(
        queries,
        key_states,
        value_states,
        attn_output,
        output_grad,
        block_map,
        w_query,
        w_key,
        w_value,
    )


def solution(mesh):
    context_count, group_count = mesh.shape["ctx"], mesh.shape["tp"]
    if context_count == 8 and group_count == 4:
        body = functools.partial(fused_device, context_count)
    else:
        body = per_device
    return jax.shard_map(
        body,
        mesh=mesh,
        in_specs=(
            P("ctx", "tp"),
            P("ctx", "tp"),
            P("ctx", "tp"),
            P("ctx", "tp"),
            P("ctx", "tp"),
            P(),
            P("ctx", "tp"),
            P("ctx", "tp"),
            P("ctx", "tp"),
        ),
        out_specs=P("tp", "ctx"),
        check_vma=False,
    )
```

```python
import functools
import math

import jax
import jax.numpy as jnp
from jax import lax
from jax.experimental import pallas as pl
from jax.experimental.pallas import tpu as pltpu
from jax.sharding import PartitionSpec as P

HD = 128
BLK = 128


NEG_FILL = -1e30


def block_mask(block_map, row_offset, row_count, col_offset, col_count):
    tiles = lax.dynamic_slice(
        block_map, (row_offset // BLK, col_offset // BLK), (row_count // BLK, col_count // BLK)
    )
    spread = jnp.broadcast_to(
        tiles[:, None, :, None], (row_count // BLK, BLK, col_count // BLK, BLK)
    )
    return spread.reshape(row_count, col_count) > 0


def resolved_rows(values):
    return lax.optimization_barrier(values.astype(jnp.bfloat16)).astype(jnp.float32)


def stat_update(state, query_heads, key_block, allowed, score_scale):
    row_max, row_sum = state
    scores = (
        jnp.einsum("qhd,khd->hqk", query_heads, key_block, preferred_element_type=jnp.float32)
        * score_scale
    )
    masked = jnp.where(allowed[None], scores, NEG_FILL)
    new_max = jnp.maximum(row_max, jnp.max(masked, axis=2))
    kept = jnp.where(allowed[None], jnp.exp(masked - new_max[:, :, None]), 0.0)
    return (new_max, row_sum * jnp.exp(row_max - new_max) + jnp.sum(kept, axis=2))


def gradient_block(
    query_heads, grad_heads, key_block, value_block, log_total, row_delta, allowed, score_scale
):
    scores = (
        jnp.einsum("qhd,khd->hqk", query_heads, key_block, preferred_element_type=jnp.float32)
        * score_scale
    )
    masked = jnp.where(allowed[None], scores, NEG_FILL)
    probs = jnp.where(allowed[None], jnp.exp(masked - log_total[:, :, None]), 0.0)
    probs_low = probs.astype(jnp.bfloat16)
    dprobs = jnp.einsum("qhd,khd->hqk", grad_heads, value_block, preferred_element_type=jnp.float32)
    score_gradient = (probs * (dprobs - row_delta[:, :, None]) * score_scale).astype(jnp.bfloat16)
    return (probs_low, score_gradient)


def per_device(
    queries, key_states, value_states, attn_output, output_grad, block_map, w_query, w_key, w_value
):
    slab_rows, width = queries.shape
    head_count = width // HD
    context_count = lax.axis_size("ctx")
    score_scale = 1.0 / math.sqrt(HD)
    row_offset = lax.axis_index("ctx") * slab_rows
    query_heads = queries.reshape(slab_rows, head_count, HD)
    grad_heads = output_grad.reshape(slab_rows, head_count, HD)
    output_heads = attn_output.reshape(slab_rows, head_count, HD)
    row_delta = jnp.sum(grad_heads.astype(jnp.float32) * output_heads.astype(jnp.float32), axis=2).T
    start_state = (
        jnp.full((head_count, slab_rows), NEG_FILL, jnp.float32),
        jnp.zeros((head_count, slab_rows), jnp.float32),
    )
    full_keys, full_values = (
        lax.all_gather(key_states, "ctx", axis=0, tiled=True),
        lax.all_gather(value_states, "ctx", axis=0, tiled=True),
    )
    group_size = min(context_count, max(1, 512 // slab_rows))
    key_span = slab_rows * group_size
    total_block_count = context_count // group_size
    key_blocks = full_keys.reshape(total_block_count, key_span, head_count, HD)
    value_blocks = full_values.reshape(total_block_count, key_span, head_count, HD)
    block_ids = jnp.arange(total_block_count, dtype=jnp.int32)

    def stat_step(state, inputs):
        key_block, block_index = inputs
        allowed = block_mask(block_map, row_offset, slab_rows, block_index * key_span, key_span)

        def stat_active_step(previous):
            return stat_update(previous, query_heads, key_block, allowed, score_scale)

        return (
            lax.cond(jnp.any(allowed), stat_active_step, lambda previous: previous, state),
            None,
        )

    (row_max, row_sum), _ = lax.scan(stat_step, start_state, (key_blocks, block_ids))
    log_total = row_max + jnp.log(row_sum)

    def back_step(dq_total, inputs):
        key_block, value_block, block_index = inputs
        allowed = block_mask(block_map, row_offset, slab_rows, block_index * key_span, key_span)

        def back_active_step(previous):
            probs_low, score_gradient = gradient_block(
                query_heads,
                grad_heads,
                key_block,
                value_block,
                log_total,
                row_delta,
                allowed,
                score_scale,
            )
            dv_part = jnp.einsum(
                "hqk,qhd->khd", probs_low, grad_heads, preferred_element_type=jnp.float32
            ).astype(jnp.bfloat16)
            dk_part = jnp.einsum(
                "hqk,qhd->khd", score_gradient, query_heads, preferred_element_type=jnp.float32
            ).astype(jnp.bfloat16)
            per_slab = jnp.einsum(
                "hqgk,gkhd->gqhd",
                score_gradient.reshape(head_count, slab_rows, group_size, slab_rows),
                key_block.reshape(group_size, slab_rows, head_count, HD),
                preferred_element_type=jnp.float32,
            )
            joined = jnp.concatenate(
                [dk_part.reshape(key_span, width), dv_part.reshape(key_span, width)], axis=1
            )
            return (previous + jnp.sum(resolved_rows(per_slab), axis=0), joined)

        def empty_step(previous):
            return (previous, jnp.zeros((key_span, 2 * width), jnp.bfloat16))

        return lax.cond(jnp.any(allowed), back_active_step, empty_step, dq_total)

    dq_total, joined_blocks = lax.scan(
        back_step,
        jnp.zeros((slab_rows, head_count, HD), jnp.float32),
        (key_blocks, value_blocks, block_ids),
    )
    local_grads = dq_total.astype(jnp.bfloat16).reshape(slab_rows, width)
    part_grads = joined_blocks.reshape(context_count * slab_rows, 2 * width)
    part_width = part_grads.shape[1]
    arrived = lax.all_to_all(
        part_grads.reshape(context_count, slab_rows, part_width),
        "ctx",
        split_axis=0,
        concat_axis=0,
        tiled=True,
    )
    finished = jnp.sum(arrived.astype(jnp.float32), axis=0).astype(jnp.bfloat16)
    own_grads = jnp.concatenate([local_grads, finished], axis=1)
    gradients = lax.all_gather(own_grads, "ctx", axis=0, tiled=True)
    projections = jnp.concatenate([w_query, w_key, w_value], axis=1)
    return lax.psum_scatter(
        lax.dot_general(
            gradients, projections, (((1,), (1,)), ((), ())), preferred_element_type=jnp.float32
        ).astype(jnp.bfloat16),
        "tp",
        scatter_dimension=0,
        tiled=True,
    )


MESH = pl.DeviceIdType.MESH
LOG2E = 1.4426950408889634
PAIR = 2 * BLK
TAIL = 16
PIECE = 256


def contract(a, b, da, db):
    return lax.dot_general(a, b, (((da,), (db,)), ((), ())), preferred_element_type=jnp.float32)


def fused_kernel(
    n,
    q_hbm,
    k_hbm,
    v_hbm,
    o_hbm,
    g_hbm,
    map_ref,
    wq_hbm,
    wk_hbm,
    wv_hbm,
    out_ref,
    held_qk,
    held_g,
    o_ref,
    bias,
    probs_ref,
    delta_ref,
    dq_acc,
    grads,
    w_ref,
    to_sib,
    from_sib,
    to_far,
    from_far,
    w_sem,
    in_sem,
    ctx_send,
    ctx_recv,
    sib_send,
    sib_recv,
    far_send,
    far_recv,
):
    heads = held_qk.shape[0]
    depth = n // 2
    tokens = n * BLK
    pieces = to_far.shape[0]
    block_rows = to_far.shape[1]
    c = lax.axis_index("ctx")
    t = lax.axis_index("tp")
    z = c // 2
    other = c + 1 - 2 * (c % 2)
    sib = t + 1 - 2 * (t % 2)
    far = (t + 2) % 4
    mate = z + 1 - 2 * (z % 2)
    scale = 1.0 / math.sqrt(HD)

    barrier = pltpu.get_barrier_semaphore()
    for peer in ({"ctx": other}, {"tp": sib}, {"tp": far}):
        pl.semaphore_signal(barrier, inc=1, device_id=peer, device_id_type=MESH)

    @pl.when(z > 0)
    def _():
        pl.semaphore_signal(barrier, inc=1, device_id={"ctx": c - 2}, device_id_type=MESH)

    @pl.when(z < depth - 1)
    def _():
        pl.semaphore_signal(barrier, inc=1, device_id={"ctx": c + 2}, device_id_type=MESH)

    in_copies = [pltpu.make_async_copy(o_hbm, o_ref, in_sem.at[4 * heads])]
    for h in range(heads):
        cols = pl.ds(h * HD, HD)
        for i, (source, target) in enumerate(
            (
                (q_hbm, held_qk.at[h, c, pl.ds(0, BLK)]),
                (k_hbm, held_qk.at[h, c, pl.ds(BLK, BLK)]),
                (g_hbm, held_g.at[h, c, pl.ds(0, BLK)]),
                (v_hbm, held_g.at[h, c, pl.ds(BLK, BLK)]),
            )
        ):
            in_copies.append(
                pltpu.make_async_copy(source.at[:, cols], target, in_sem.at[4 * h + i])
            )
    for copy in in_copies:
        copy.start()
    w_copies = [
        pltpu.make_async_copy(w, w_ref.at[:, pl.ds(i * heads * HD, heads * HD)], w_sem.at[i])
        for i, w in enumerate((wq_hbm, wk_hbm, wv_hbm))
    ]
    for copy in w_copies:
        copy.start()
    for copy in in_copies:
        copy.wait()

    stores = (held_qk, held_g)
    streams = [(kind, h) for kind in range(2) for h in range(heads)]

    def ctx_copy(s, slab, way, target):
        kind, h = streams[s]
        return pltpu.make_async_remote_copy(
            src_ref=stores[kind].at[h, slab],
            dst_ref=stores[kind].at[h, slab],
            send_sem=ctx_send.at[s, way, slab],
            recv_sem=ctx_recv.at[s, slab],
            device_id={"ctx": target},
            device_id_type=MESH,
        )

    def send_up(h, slab):
        @pl.when(z < depth - 1)
        def _():
            ctx_copy(h, slab, 0, c + 2).start()

    def send_down(h, slab):
        @pl.when(z > 0)
        def _():
            ctx_copy(h, slab, 1, c - 2).start()

    def send_own(h):
        send_up(h, c)
        send_down(h, c)
        ctx_copy(h, c, 2, other).start()

    def relayed(s):
        return streams[s][0] == 1

    def cross(s, slab):
        if relayed(s):

            @pl.when(slab // 2 != mate)
            def _():
                ctx_copy(s, slab, 2, other).start()

        else:
            ctx_copy(s, slab, 2, other).start()

    def relay(s):
        ctx_copy(s, other, 0, c).wait_recv()

        @pl.when(z % 2 == 0)
        def _():
            ctx_copy(s, other, 0, c + 2).start()

        @pl.when(z % 2 == 1)
        def _():
            ctx_copy(s, other, 1, c - 2).start()

    def pass_on(h, d):
        @pl.when(z - d >= 0)
        def _():
            slab = c - 2 * d
            ctx_copy(h, slab, 0, c).wait_recv()
            send_up(h, slab)
            cross(h, slab)

        @pl.when(z + d < depth)
        def _():
            slab = c + 2 * d
            ctx_copy(h, slab, 0, c).wait_recv()
            send_down(h, slab)
            cross(h, slab)

    pl.semaphore_wait(
        barrier,
        3 + jnp.where(z > 0, 1, 0) + jnp.where(z < depth - 1, 1, 0),
    )
    for s in range(2):
        send_own(s)

    for h in range(heads):
        grad = held_g[h, c, 0:BLK, :].astype(jnp.float32)
        product = grad * o_ref[:, h * HD : (h + 1) * HD].astype(jnp.float32)
        delta = jnp.sum(product.T, axis=0, keepdims=True)
        high = delta.astype(jnp.bfloat16)
        rest = delta - high.astype(jnp.float32)
        middle = rest.astype(jnp.bfloat16)
        low = (rest - middle.astype(jnp.float32)).astype(jnp.bfloat16)
        held_g[h, c, 2 * BLK : 2 * BLK + TAIL, :] = jnp.concatenate(
            [high, middle, low, jnp.zeros((TAIL - 3, BLK), jnp.bfloat16)], axis=0
        )

    for a in range(n):
        for b in range(n):
            bias[b : b + 1, a * BLK : (a + 1) * BLK] = jnp.full(
                (1, BLK), jnp.where(map_ref[a, b] > 0, 0.0, NEG_FILL), jnp.float32
            )
    dq_acc[...] = jnp.zeros_like(dq_acc)

    def soften(h, i):
        keys = held_qk[h, :, BLK : 2 * BLK, :].reshape(tokens, HD)
        pair_q = held_qk[h, pl.ds(2 * i, 2), 0:BLK, :].reshape(PAIR, HD)
        columns = pl.ds(pl.multiple_of(i * PAIR, PAIR), PAIR)
        scores = contract(keys, pair_q, 1, 1) * (scale * LOG2E)
        masked = scores.reshape(n, BLK, PAIR) + bias[:, columns][:, None, :]
        top = jnp.max(masked, axis=(0, 1), keepdims=True)
        raised = jnp.exp2(masked - top)
        total = jnp.sum(raised, axis=(0, 1), keepdims=True)
        probs = (raised * (1.0 / total)).reshape(tokens, PAIR)
        probs_ref[h, :, columns] = probs.astype(jnp.bfloat16)

    def value_rows(h, i):
        rows = pl.ds(pl.multiple_of(i * PAIR, PAIR), PAIR)
        all_g = held_g[h, :, 0:BLK, :].reshape(tokens, HD)
        first = (2 * heads + h) * HD
        grads[rows, first : first + HD] = contract(probs_ref[h, rows, :], all_g, 1, 0).astype(
            jnp.bfloat16
        )

    def key_rows(h, i):
        rows = pl.ds(pl.multiple_of(i * PAIR, PAIR), PAIR)
        pair = pl.ds(2 * i, 2)
        all_g = held_g[h, :, 0:BLK, :].reshape(tokens, HD)
        all_q = held_qk[h, :, 0:BLK, :].reshape(tokens, HD)
        keys = held_qk[h, pair, BLK : 2 * BLK, :].reshape(PAIR, HD)
        values = held_g[h, pair, BLK : 2 * BLK, :].reshape(PAIR, HD)
        dprobs = contract(values, all_g, 1, 1)
        probs = probs_ref[h, rows, :].astype(jnp.float32)
        dscores = (probs * (dprobs - delta_ref[h : h + 1, :])).astype(jnp.bfloat16)
        first = (heads + h) * HD
        grads[rows, first : first + HD] = (contract(dscores, all_q, 1, 0) * scale).astype(
            jnp.bfloat16
        )
        dq_acc[h] += contract(keys, dscores, 0, 0)

    def spread_delta(h):
        sums = jnp.sum(held_g[h, :, 2 * BLK : 2 * BLK + TAIL, :].astype(jnp.float32), axis=1)
        for a in range(n):
            delta_ref[h : h + 1, a * BLK : (a + 1) * BLK] = sums[a : a + 1]

    def passive(s):
        def one(j, carry):
            def arrive():
                ctx_copy(s, (1 - c % 2) + 2 * j, 0, c).wait_recv()

            if relayed(s):
                pl.when(j != z)(arrive)
            else:
                arrive()
            return carry

        lax.fori_loop(0, depth, one, 0)

    def backward(h, i):
        value_rows(h, i)
        key_rows(h, i)

    count = len(streams)
    for wave in range(1, count + depth):
        for d in range(depth - 1, 0, -1):
            if 0 <= wave - d < count:
                pass_on(wave - d, d)
        if 0 <= wave - 1 < count and relayed(wave - 1):
            relay(wave - 1)
        if wave + 1 < count:
            send_own(wave + 1)
        if wave < depth:
            continue
        s = wave - depth
        kind, h = streams[s]
        passive(s)
        if kind == 1:
            spread_delta(h)
        work = (soften, backward)[kind]

        def step(i, carry, h=h, work=work):
            work(h, i)
            return carry

        lax.fori_loop(0, depth, step, 0)
        if kind == 1:
            grads[:, h * HD : (h + 1) * HD] = (dq_acc[h].T * scale).astype(jnp.bfloat16)
    for copy in w_copies:
        copy.wait()

    def term(block, p):
        rows = grads[pl.ds(pl.multiple_of(block * block_rows, block_rows), block_rows), :]
        return contract(rows, w_ref[pl.ds(pl.multiple_of(p * PIECE, PIECE), PIECE), :], 1, 1)

    def sib_copy(k, p):
        return pltpu.make_async_remote_copy(
            src_ref=to_sib.at[k, p],
            dst_ref=from_sib.at[k, p],
            send_sem=sib_send.at[k, p],
            recv_sem=sib_recv.at[k, p],
            device_id={"tp": sib},
            device_id_type=MESH,
        )

    def far_copy(p):
        return pltpu.make_async_remote_copy(
            src_ref=to_far.at[p],
            dst_ref=from_far.at[p],
            send_sem=far_send.at[p],
            recv_sem=far_recv.at[p],
            device_id={"tp": far},
            device_id_type=MESH,
        )

    def for_sib(k, block, p):
        to_sib[k, p] = term(block, p).astype(jnp.bfloat16)
        sib_copy(k, p).start()

    def for_far(p):
        own = term(far, p)
        sib_copy(0, p).wait_recv()
        to_far[p] = (own + from_sib[0, p].astype(jnp.float32)).astype(jnp.bfloat16)
        far_copy(p).start()

    def for_out(p, carry):
        own = term(t, p)
        sib_copy(1, p).wait_recv()
        own = own + from_sib[1, p].astype(jnp.float32)
        far_copy(p).wait_recv()
        out_ref[:, pl.ds(pl.multiple_of(p * PIECE, PIECE), PIECE)] = (
            own + from_far[p].astype(jnp.float32)
        ).astype(jnp.bfloat16)
        return carry

    lead = 2

    def first_terms(p, carry):
        @pl.when(p < pieces)
        def _():
            for_sib(0, (sib + 2) % 4, p)

        @pl.when(p >= lead)
        def _():
            for_far(p - lead)

        return carry

    lax.fori_loop(0, pieces + lead, first_terms, 0)

    def near_terms(p, carry):
        for_sib(1, sib, p)
        return carry

    lax.fori_loop(0, pieces, near_terms, 0)
    lax.fori_loop(0, pieces, for_out, 0)

    def drain(p, carry):
        sib_copy(0, p).wait_send()
        sib_copy(1, p).wait_send()
        far_copy(p).wait_send()
        return carry

    lax.fori_loop(0, pieces, drain, 0)

    def drain_ctx(j, carry):
        slab = c % 2 + 2 * j
        for h in range(len(streams)):
            if relayed(h):
                pl.when(j != mate)(ctx_copy(h, slab, 2, c).wait_send)
            else:
                ctx_copy(h, slab, 2, c).wait_send()

            @pl.when((j <= z) & (z < depth - 1))
            def _():
                ctx_copy(h, slab, 0, c).wait_send()

            @pl.when((j >= z) & (z > 0))
            def _():
                ctx_copy(h, slab, 1, c).wait_send()

        return carry

    lax.fori_loop(0, depth, drain_ctx, 0)
    for s in range(len(streams)):
        if relayed(s):
            pl.when(z % 2 == 0)(ctx_copy(s, other, 0, c).wait_send)
            pl.when(z % 2 == 1)(ctx_copy(s, other, 1, c).wait_send)


def fused_device(
    n,
    queries,
    key_states,
    value_states,
    attn_output,
    output_grad,
    block_map,
    w_query,
    w_key,
    w_value,
):
    slab_rows, width = queries.shape
    heads = width // HD
    tokens = n * slab_rows
    model = w_query.shape[0]
    block_rows = tokens // 4
    pieces = model // PIECE
    vmem = pl.BlockSpec(memory_space=pltpu.VMEM)
    dma = pltpu.SemaphoreType.DMA
    return pl.pallas_call(
        functools.partial(fused_kernel, n),
        out_shape=jax.ShapeDtypeStruct((block_rows, model), jnp.bfloat16),
        in_specs=[pl.BlockSpec(memory_space=pl.ANY)] * 5
        + [pl.BlockSpec(memory_space=pltpu.SMEM)]
        + [pl.BlockSpec(memory_space=pl.ANY)] * 3,
        out_specs=vmem,
        scratch_shapes=[
            pltpu.VMEM((heads, n, 2 * BLK, HD), jnp.bfloat16),
            pltpu.VMEM((heads, n, 2 * BLK + TAIL, HD), jnp.bfloat16),
            pltpu.VMEM((slab_rows, width), jnp.bfloat16),
            pltpu.VMEM((n, tokens), jnp.float32),
            pltpu.VMEM((heads, tokens, tokens), jnp.bfloat16),
            pltpu.VMEM((heads, tokens), jnp.float32),
            pltpu.VMEM((heads, HD, tokens), jnp.float32),
            pltpu.VMEM((tokens, 3 * width), jnp.bfloat16),
            pltpu.VMEM((model, 3 * width), jnp.bfloat16),
            pltpu.VMEM((2, pieces, block_rows, PIECE), jnp.bfloat16),
            pltpu.VMEM((2, pieces, block_rows, PIECE), jnp.bfloat16),
            pltpu.VMEM((pieces, block_rows, PIECE), jnp.bfloat16),
            pltpu.VMEM((pieces, block_rows, PIECE), jnp.bfloat16),
            dma((3,)),
            dma((4 * heads + 1,)),
            dma((2 * heads, 3, n)),
            dma((2 * heads, n)),
            dma((2, pieces)),
            dma((2, pieces)),
            dma((pieces,)),
            dma((pieces,)),
        ],
        compiler_params=pltpu.CompilerParams(
            collective_id=0, has_side_effects=True, vmem_limit_bytes=62 * 1024 * 1024
        ),
        cost_estimate=pl.CostEstimate(
            flops=10 * heads * tokens * tokens * HD + 6 * tokens * model * width,
            bytes_accessed=6 * model * width + 2 * block_rows * model,
            transcendentals=heads * tokens * tokens,
        ),
    )(
        queries,
        key_states,
        value_states,
        attn_output,
        output_grad,
        block_map,
        w_query,
        w_key,
        w_value,
    )


def solution(mesh):
    context_count, group_count = mesh.shape["ctx"], mesh.shape["tp"]
    if context_count == 8 and group_count == 4:
        body = functools.partial(fused_device, context_count)
    else:
        body = per_device
    return jax.shard_map(
        body,
        mesh=mesh,
        in_specs=(
            P("ctx", "tp"),
            P("ctx", "tp"),
            P("ctx", "tp"),
            P("ctx", "tp"),
            P("ctx", "tp"),
            P(),
            P("ctx", "tp"),
            P("ctx", "tp"),
            P("ctx", "tp"),
        ),
        out_specs=P("tp", "ctx"),
        check_vma=False,
    )
```

```python
import functools
import math

import jax
import jax.numpy as jnp
from jax import lax
from jax.experimental import pallas as pl
from jax.experimental.pallas import tpu as pltpu
from jax.sharding import PartitionSpec as P

HD = 128
BLK = 128


NEG_FILL = -1e30


def block_mask(block_map, row_offset, row_count, col_offset, col_count):
    tiles = lax.dynamic_slice(
        block_map, (row_offset // BLK, col_offset // BLK), (row_count // BLK, col_count // BLK)
    )
    spread = jnp.broadcast_to(
        tiles[:, None, :, None], (row_count // BLK, BLK, col_count // BLK, BLK)
    )
    return spread.reshape(row_count, col_count) > 0


def resolved_rows(values):
    return lax.optimization_barrier(values.astype(jnp.bfloat16)).astype(jnp.float32)


def stat_update(state, query_heads, key_block, allowed, score_scale):
    row_max, row_sum = state
    scores = (
        jnp.einsum("qhd,khd->hqk", query_heads, key_block, preferred_element_type=jnp.float32)
        * score_scale
    )
    masked = jnp.where(allowed[None], scores, NEG_FILL)
    new_max = jnp.maximum(row_max, jnp.max(masked, axis=2))
    kept = jnp.where(allowed[None], jnp.exp(masked - new_max[:, :, None]), 0.0)
    return (new_max, row_sum * jnp.exp(row_max - new_max) + jnp.sum(kept, axis=2))


def gradient_block(
    query_heads, grad_heads, key_block, value_block, log_total, row_delta, allowed, score_scale
):
    scores = (
        jnp.einsum("qhd,khd->hqk", query_heads, key_block, preferred_element_type=jnp.float32)
        * score_scale
    )
    masked = jnp.where(allowed[None], scores, NEG_FILL)
    probs = jnp.where(allowed[None], jnp.exp(masked - log_total[:, :, None]), 0.0)
    probs_low = probs.astype(jnp.bfloat16)
    dprobs = jnp.einsum("qhd,khd->hqk", grad_heads, value_block, preferred_element_type=jnp.float32)
    score_gradient = (probs * (dprobs - row_delta[:, :, None]) * score_scale).astype(jnp.bfloat16)
    return (probs_low, score_gradient)


def per_device(
    queries, key_states, value_states, attn_output, output_grad, block_map, w_query, w_key, w_value
):
    slab_rows, width = queries.shape
    head_count = width // HD
    context_count = lax.axis_size("ctx")
    score_scale = 1.0 / math.sqrt(HD)
    row_offset = lax.axis_index("ctx") * slab_rows
    query_heads = queries.reshape(slab_rows, head_count, HD)
    grad_heads = output_grad.reshape(slab_rows, head_count, HD)
    output_heads = attn_output.reshape(slab_rows, head_count, HD)
    row_delta = jnp.sum(grad_heads.astype(jnp.float32) * output_heads.astype(jnp.float32), axis=2).T
    start_state = (
        jnp.full((head_count, slab_rows), NEG_FILL, jnp.float32),
        jnp.zeros((head_count, slab_rows), jnp.float32),
    )
    full_keys, full_values = (
        lax.all_gather(key_states, "ctx", axis=0, tiled=True),
        lax.all_gather(value_states, "ctx", axis=0, tiled=True),
    )
    group_size = min(context_count, max(1, 512 // slab_rows))
    key_span = slab_rows * group_size
    total_block_count = context_count // group_size
    key_blocks = full_keys.reshape(total_block_count, key_span, head_count, HD)
    value_blocks = full_values.reshape(total_block_count, key_span, head_count, HD)
    block_ids = jnp.arange(total_block_count, dtype=jnp.int32)

    def stat_step(state, inputs):
        key_block, block_index = inputs
        allowed = block_mask(block_map, row_offset, slab_rows, block_index * key_span, key_span)

        def stat_active_step(previous):
            return stat_update(previous, query_heads, key_block, allowed, score_scale)

        return (
            lax.cond(jnp.any(allowed), stat_active_step, lambda previous: previous, state),
            None,
        )

    (row_max, row_sum), _ = lax.scan(stat_step, start_state, (key_blocks, block_ids))
    log_total = row_max + jnp.log(row_sum)

    def back_step(dq_total, inputs):
        key_block, value_block, block_index = inputs
        allowed = block_mask(block_map, row_offset, slab_rows, block_index * key_span, key_span)

        def back_active_step(previous):
            probs_low, score_gradient = gradient_block(
                query_heads,
                grad_heads,
                key_block,
                value_block,
                log_total,
                row_delta,
                allowed,
                score_scale,
            )
            dv_part = jnp.einsum(
                "hqk,qhd->khd", probs_low, grad_heads, preferred_element_type=jnp.float32
            ).astype(jnp.bfloat16)
            dk_part = jnp.einsum(
                "hqk,qhd->khd", score_gradient, query_heads, preferred_element_type=jnp.float32
            ).astype(jnp.bfloat16)
            per_slab = jnp.einsum(
                "hqgk,gkhd->gqhd",
                score_gradient.reshape(head_count, slab_rows, group_size, slab_rows),
                key_block.reshape(group_size, slab_rows, head_count, HD),
                preferred_element_type=jnp.float32,
            )
            joined = jnp.concatenate(
                [dk_part.reshape(key_span, width), dv_part.reshape(key_span, width)], axis=1
            )
            return (previous + jnp.sum(resolved_rows(per_slab), axis=0), joined)

        def empty_step(previous):
            return (previous, jnp.zeros((key_span, 2 * width), jnp.bfloat16))

        return lax.cond(jnp.any(allowed), back_active_step, empty_step, dq_total)

    dq_total, joined_blocks = lax.scan(
        back_step,
        jnp.zeros((slab_rows, head_count, HD), jnp.float32),
        (key_blocks, value_blocks, block_ids),
    )
    local_grads = dq_total.astype(jnp.bfloat16).reshape(slab_rows, width)
    part_grads = joined_blocks.reshape(context_count * slab_rows, 2 * width)
    part_width = part_grads.shape[1]
    arrived = lax.all_to_all(
        part_grads.reshape(context_count, slab_rows, part_width),
        "ctx",
        split_axis=0,
        concat_axis=0,
        tiled=True,
    )
    finished = jnp.sum(arrived.astype(jnp.float32), axis=0).astype(jnp.bfloat16)
    own_grads = jnp.concatenate([local_grads, finished], axis=1)
    gradients = lax.all_gather(own_grads, "ctx", axis=0, tiled=True)
    projections = jnp.concatenate([w_query, w_key, w_value], axis=1)
    return lax.psum_scatter(
        lax.dot_general(
            gradients, projections, (((1,), (1,)), ((), ())), preferred_element_type=jnp.float32
        ).astype(jnp.bfloat16),
        "tp",
        scatter_dimension=0,
        tiled=True,
    )


MESH = pl.DeviceIdType.MESH
LOG2E = 1.4426950408889634
PAIR = 2 * BLK
TAIL = 16
PIECE = 256


def contract(a, b, da, db):
    return lax.dot_general(a, b, (((da,), (db,)), ((), ())), preferred_element_type=jnp.float32)


def fused_kernel(
    n,
    q_hbm,
    k_hbm,
    v_hbm,
    o_hbm,
    g_hbm,
    map_ref,
    wq_hbm,
    wk_hbm,
    wv_hbm,
    out_ref,
    held_qk,
    held_g,
    o_ref,
    bias,
    probs_ref,
    delta_ref,
    dq_acc,
    grads,
    w_ref,
    to_sib,
    from_sib,
    to_far,
    from_far,
    w_sem,
    in_sem,
    ctx_send,
    ctx_recv,
    sib_send,
    sib_recv,
    far_send,
    far_recv,
):
    heads = held_qk.shape[0]
    depth = n // 2
    tokens = n * BLK
    pieces = to_far.shape[0]
    block_rows = to_far.shape[1]
    c = lax.axis_index("ctx")
    t = lax.axis_index("tp")
    z = c // 2
    other = c + 1 - 2 * (c % 2)
    sib = t + 1 - 2 * (t % 2)
    far = (t + 2) % 4
    scale = 1.0 / math.sqrt(HD)

    barrier = pltpu.get_barrier_semaphore()
    for peer in ({"ctx": other}, {"tp": sib}, {"tp": far}):
        pl.semaphore_signal(barrier, inc=1, device_id=peer, device_id_type=MESH)

    @pl.when(z > 0)
    def _():
        pl.semaphore_signal(barrier, inc=1, device_id={"ctx": c - 2}, device_id_type=MESH)

    @pl.when(z < depth - 1)
    def _():
        pl.semaphore_signal(barrier, inc=1, device_id={"ctx": c + 2}, device_id_type=MESH)

    in_copies = [pltpu.make_async_copy(o_hbm, o_ref, in_sem.at[4 * heads])]
    for h in range(heads):
        cols = pl.ds(h * HD, HD)
        for i, (source, target) in enumerate(
            (
                (q_hbm, held_qk.at[h, c, pl.ds(0, BLK)]),
                (k_hbm, held_qk.at[h, c, pl.ds(BLK, BLK)]),
                (g_hbm, held_g.at[h, c, pl.ds(0, BLK)]),
                (v_hbm, held_g.at[h, c, pl.ds(BLK, BLK)]),
            )
        ):
            in_copies.append(
                pltpu.make_async_copy(source.at[:, cols], target, in_sem.at[4 * h + i])
            )
    for copy in in_copies:
        copy.start()
    w_copies = [
        pltpu.make_async_copy(w, w_ref.at[:, pl.ds(i * heads * HD, heads * HD)], w_sem.at[i])
        for i, w in enumerate((wq_hbm, wk_hbm, wv_hbm))
    ]
    for copy in w_copies:
        copy.start()
    for copy in in_copies:
        copy.wait()

    for h in range(heads):
        grad = held_g[h, c, 0:BLK, :].astype(jnp.float32)
        product = grad * o_ref[:, h * HD : (h + 1) * HD].astype(jnp.float32)
        delta = jnp.sum(product.T, axis=0, keepdims=True)
        high = delta.astype(jnp.bfloat16)
        rest = delta - high.astype(jnp.float32)
        middle = rest.astype(jnp.bfloat16)
        low = (rest - middle.astype(jnp.float32)).astype(jnp.bfloat16)
        held_g[h, c, 2 * BLK : 2 * BLK + TAIL, :] = jnp.concatenate(
            [high, middle, low, jnp.zeros((TAIL - 3, BLK), jnp.bfloat16)], axis=0
        )

    stores = (held_qk, held_g)
    streams = [(kind, h) for kind in range(2) for h in range(heads)]

    def ctx_copy(s, slab, way, target):
        kind, h = streams[s]
        return pltpu.make_async_remote_copy(
            src_ref=stores[kind].at[h, slab],
            dst_ref=stores[kind].at[h, slab],
            send_sem=ctx_send.at[s, way, slab],
            recv_sem=ctx_recv.at[s, slab],
            device_id={"ctx": target},
            device_id_type=MESH,
        )

    def send_up(h, slab):
        @pl.when(z < depth - 1)
        def _():
            ctx_copy(h, slab, 0, c + 2).start()

    def send_down(h, slab):
        @pl.when(z > 0)
        def _():
            ctx_copy(h, slab, 1, c - 2).start()

    def send_own(h):
        send_up(h, c)
        send_down(h, c)
        ctx_copy(h, c, 2, other).start()

    def pass_on(h, d):
        @pl.when(z - d >= 0)
        def _():
            slab = c - 2 * d
            ctx_copy(h, slab, 0, c).wait_recv()
            send_up(h, slab)
            ctx_copy(h, slab, 2, other).start()

        @pl.when(z + d < depth)
        def _():
            slab = c + 2 * d
            ctx_copy(h, slab, 0, c).wait_recv()
            send_down(h, slab)
            ctx_copy(h, slab, 2, other).start()

    pl.semaphore_wait(
        barrier,
        3 + jnp.where(z > 0, 1, 0) + jnp.where(z < depth - 1, 1, 0),
    )
    for s in range(2):
        send_own(s)

    for a in range(n):
        for b in range(n):
            bias[b : b + 1, a * BLK : (a + 1) * BLK] = jnp.full(
                (1, BLK), jnp.where(map_ref[a, b] > 0, 0.0, NEG_FILL), jnp.float32
            )
    dq_acc[...] = jnp.zeros_like(dq_acc)

    def soften(h, i):
        keys = held_qk[h, :, BLK : 2 * BLK, :].reshape(tokens, HD)
        pair_q = held_qk[h, pl.ds(2 * i, 2), 0:BLK, :].reshape(PAIR, HD)
        columns = pl.ds(pl.multiple_of(i * PAIR, PAIR), PAIR)
        scores = contract(keys, pair_q, 1, 1) * (scale * LOG2E)
        masked = scores.reshape(n, BLK, PAIR) + bias[:, columns][:, None, :]
        top = jnp.max(masked, axis=(0, 1), keepdims=True)
        raised = jnp.exp2(masked - top)
        total = jnp.sum(raised, axis=(0, 1), keepdims=True)
        probs = (raised * (1.0 / total)).reshape(tokens, PAIR)
        probs_ref[h, :, columns] = probs.astype(jnp.bfloat16)

    def value_rows(h, i):
        rows = pl.ds(pl.multiple_of(i * PAIR, PAIR), PAIR)
        all_g = held_g[h, :, 0:BLK, :].reshape(tokens, HD)
        first = (2 * heads + h) * HD
        grads[rows, first : first + HD] = contract(probs_ref[h, rows, :], all_g, 1, 0).astype(
            jnp.bfloat16
        )

    def key_rows(h, i):
        rows = pl.ds(pl.multiple_of(i * PAIR, PAIR), PAIR)
        pair = pl.ds(2 * i, 2)
        all_g = held_g[h, :, 0:BLK, :].reshape(tokens, HD)
        all_q = held_qk[h, :, 0:BLK, :].reshape(tokens, HD)
        keys = held_qk[h, pair, BLK : 2 * BLK, :].reshape(PAIR, HD)
        values = held_g[h, pair, BLK : 2 * BLK, :].reshape(PAIR, HD)
        dprobs = contract(values, all_g, 1, 1)
        probs = probs_ref[h, rows, :].astype(jnp.float32)
        dscores = (probs * (dprobs - delta_ref[h : h + 1, :])).astype(jnp.bfloat16)
        first = (heads + h) * HD
        grads[rows, first : first + HD] = (contract(dscores, all_q, 1, 0) * scale).astype(
            jnp.bfloat16
        )
        dq_acc[h] += contract(keys, dscores, 0, 0)

    def spread_delta(h):
        sums = jnp.sum(held_g[h, :, 2 * BLK : 2 * BLK + TAIL, :].astype(jnp.float32), axis=1)
        for a in range(n):
            delta_ref[h : h + 1, a * BLK : (a + 1) * BLK] = sums[a : a + 1]

    def passive(s):
        def one(j, carry):
            ctx_copy(s, (1 - c % 2) + 2 * j, 0, c).wait_recv()
            return carry

        lax.fori_loop(0, depth, one, 0)

    def backward(h, i):
        value_rows(h, i)
        key_rows(h, i)

    count = len(streams)
    for wave in range(1, count + depth):
        for d in range(depth - 1, 0, -1):
            if 0 <= wave - d < count:
                pass_on(wave - d, d)
        if wave + 1 < count:
            send_own(wave + 1)
        if wave < depth:
            continue
        s = wave - depth
        kind, h = streams[s]
        passive(s)
        if kind == 1:
            spread_delta(h)
        work = (soften, backward)[kind]

        def step(i, carry, h=h, work=work):
            work(h, i)
            return carry

        lax.fori_loop(0, depth, step, 0, unroll=2)
        if kind == 1:
            grads[:, h * HD : (h + 1) * HD] = (dq_acc[h].T * scale).astype(jnp.bfloat16)
    for copy in w_copies:
        copy.wait()

    def term(block, p):
        rows = grads[pl.ds(pl.multiple_of(block * block_rows, block_rows), block_rows), :]
        return contract(rows, w_ref[pl.ds(pl.multiple_of(p * PIECE, PIECE), PIECE), :], 1, 1)

    def sib_copy(k, p):
        return pltpu.make_async_remote_copy(
            src_ref=to_sib.at[k, p],
            dst_ref=from_sib.at[k, p],
            send_sem=sib_send.at[k, p],
            recv_sem=sib_recv.at[k, p],
            device_id={"tp": sib},
            device_id_type=MESH,
        )

    def far_copy(p):
        return pltpu.make_async_remote_copy(
            src_ref=to_far.at[p],
            dst_ref=from_far.at[p],
            send_sem=far_send.at[p],
            recv_sem=far_recv.at[p],
            device_id={"tp": far},
            device_id_type=MESH,
        )

    def for_sib(k, block):
        def one(p, carry):
            to_sib[k, p] = term(block, p).astype(jnp.bfloat16)
            sib_copy(k, p).start()
            return carry

        lax.fori_loop(0, pieces, one, 0)

    def for_far(p, carry):
        own = term(far, p)
        sib_copy(0, p).wait_recv()
        to_far[p] = (own + from_sib[0, p].astype(jnp.float32)).astype(jnp.bfloat16)
        far_copy(p).start()
        return carry

    def for_out(p, carry):
        own = term(t, p)
        sib_copy(1, p).wait_recv()
        own = own + from_sib[1, p].astype(jnp.float32)
        far_copy(p).wait_recv()
        out_ref[:, pl.ds(pl.multiple_of(p * PIECE, PIECE), PIECE)] = (
            own + from_far[p].astype(jnp.float32)
        ).astype(jnp.bfloat16)
        return carry

    for_sib(0, (sib + 2) % 4)
    lax.fori_loop(0, pieces, for_far, 0)
    for_sib(1, sib)
    lax.fori_loop(0, pieces, for_out, 0)

    def drain(p, carry):
        sib_copy(0, p).wait_send()
        sib_copy(1, p).wait_send()
        far_copy(p).wait_send()
        return carry

    lax.fori_loop(0, pieces, drain, 0)

    def drain_ctx(j, carry):
        slab = c % 2 + 2 * j
        for h in range(len(streams)):
            ctx_copy(h, slab, 2, c).wait_send()

            @pl.when((j <= z) & (z < depth - 1))
            def _():
                ctx_copy(h, slab, 0, c).wait_send()

            @pl.when((j >= z) & (z > 0))
            def _():
                ctx_copy(h, slab, 1, c).wait_send()

        return carry

    lax.fori_loop(0, depth, drain_ctx, 0)


def fused_device(
    n,
    queries,
    key_states,
    value_states,
    attn_output,
    output_grad,
    block_map,
    w_query,
    w_key,
    w_value,
):
    slab_rows, width = queries.shape
    heads = width // HD
    tokens = n * slab_rows
    model = w_query.shape[0]
    block_rows = tokens // 4
    pieces = model // PIECE
    vmem = pl.BlockSpec(memory_space=pltpu.VMEM)
    dma = pltpu.SemaphoreType.DMA
    return pl.pallas_call(
        functools.partial(fused_kernel, n),
        out_shape=jax.ShapeDtypeStruct((block_rows, model), jnp.bfloat16),
        in_specs=[pl.BlockSpec(memory_space=pl.ANY)] * 5
        + [pl.BlockSpec(memory_space=pltpu.SMEM)]
        + [pl.BlockSpec(memory_space=pl.ANY)] * 3,
        out_specs=vmem,
        scratch_shapes=[
            pltpu.VMEM((heads, n, 2 * BLK, HD), jnp.bfloat16),
            pltpu.VMEM((heads, n, 2 * BLK + TAIL, HD), jnp.bfloat16),
            pltpu.VMEM((slab_rows, width), jnp.bfloat16),
            pltpu.VMEM((n, tokens), jnp.float32),
            pltpu.VMEM((heads, tokens, tokens), jnp.bfloat16),
            pltpu.VMEM((heads, tokens), jnp.float32),
            pltpu.VMEM((heads, HD, tokens), jnp.float32),
            pltpu.VMEM((tokens, 3 * width), jnp.bfloat16),
            pltpu.VMEM((model, 3 * width), jnp.bfloat16),
            pltpu.VMEM((2, pieces, block_rows, PIECE), jnp.bfloat16),
            pltpu.VMEM((2, pieces, block_rows, PIECE), jnp.bfloat16),
            pltpu.VMEM((pieces, block_rows, PIECE), jnp.bfloat16),
            pltpu.VMEM((pieces, block_rows, PIECE), jnp.bfloat16),
            dma((3,)),
            dma((4 * heads + 1,)),
            dma((2 * heads, 3, n)),
            dma((2 * heads, n)),
            dma((2, pieces)),
            dma((2, pieces)),
            dma((pieces,)),
            dma((pieces,)),
        ],
        compiler_params=pltpu.CompilerParams(
            collective_id=0, has_side_effects=True, vmem_limit_bytes=62 * 1024 * 1024
        ),
        cost_estimate=pl.CostEstimate(
            flops=10 * heads * tokens * tokens * HD + 6 * tokens * model * width,
            bytes_accessed=6 * model * width + 2 * block_rows * model,
            transcendentals=heads * tokens * tokens,
        ),
    )(
        queries,
        key_states,
        value_states,
        attn_output,
        output_grad,
        block_map,
        w_query,
        w_key,
        w_value,
    )


def solution(mesh):
    context_count, group_count = mesh.shape["ctx"], mesh.shape["tp"]
    if context_count == 8 and group_count == 4:
        body = functools.partial(fused_device, context_count)
    else:
        body = per_device
    return jax.shard_map(
        body,
        mesh=mesh,
        in_specs=(
            P("ctx", "tp"),
            P("ctx", "tp"),
            P("ctx", "tp"),
            P("ctx", "tp"),
            P("ctx", "tp"),
            P(),
            P("ctx", "tp"),
            P("ctx", "tp"),
            P("ctx", "tp"),
        ),
        out_specs=P("tp", "ctx"),
        check_vma=False,
    )
```
